32 devices in a mesh: dp: 4 (over y, x), expert: 8 (over z, core).
Axes of the slice: x: 2, y: 2, z: 4, core: 2. Of those that a mesh axis runs over, the one named last changes fastest.
Arguments:
- latent: bfloat16 [4096, 1024], P(('dp', 'expert')), may hold values from -6 to 6
- cotangent: bfloat16 [4096, 1024], P(('dp', 'expert')), may hold values from -0.59765625 to 0.59765625
- routes: int32 [4096, 1], P(('dp', 'expert')), may hold values from 0 to 7; in each aligned block of 128 rows (0 to 127, 128 to 255, ...) at most 32 rows name the same one
- gates: float32 [4096, 1], P(('dp', 'expert')), may hold values from 0.1 to 1
- w_in: bfloat16 [8, 1024, 2048], P('expert'), may hold values from -0.1875 to 0.1875
- w_out: bfloat16 [8, 1024, 1024], P('expert'), may hold values from -0.1875 to 0.1875
Outputs:
- output: bfloat16 [4096, 1024], P(('dp', 'expert'))
- grad_in: float32 [8, 1024, 2048], P('expert', 'dp')
- grad_out: float32 [8, 1024, 1024], P('expert', 'dp')
The draws below stay inside these ranges and needn't reach their ends.
Inputs may be any that keep to these rules, and one draw needn't show every extreme that they name: In each aligned block of 128 tokens no expert is named by more than 32 routes, a bound that some block reaches.
All inputs are finite; a program needn't handle non-finite values.
Results may differ from the reference program's by a relative error of at most 0.018.
Values may be sent and summed in bfloat16 or wider, within the bound.
A program may use at most 64 MiB of HBM per device.

```python
import math
import jax
import jax.numpy as jnp
import numpy as np
from jax import lax

L = 1024
H = 1024
T_DEV = 128
TOP = 1
EXPERTS = 8
CAP = 32
TOKENS = 4096
N_DP = 4
N_EXPERT = 8


def level_of(rng, shape, cuts, low, largest):
    gain, own = 1.0, jax.random.fold_in(rng, 6)
    for axis_at, parts in cuts:
        heights = jnp.exp(jax.random.uniform(jax.random.fold_in(own, axis_at), (parts,), jnp.float32, low / len(cuts), largest / len(cuts)))
        gain = gain * jnp.repeat(heights, shape[axis_at] // parts).reshape([-1 if axis == axis_at else 1 for axis in range(len(shape))])
    return gain


def assign_block(key, own, number, rows, number_of, top, bound, lean):
    sequence = jax.random.permutation(key, number_of)
    heavy_load, common = shares(number_of, rows * top, bound, lean, True), shares(number_of, rows * top, bound, lean, False)
    places = jnp.arange(number_of)

    def named(sizes, turn):
        used = int((sizes > 0).sum())
        fixed = max(1, used // 4)
        shifted = fixed + (places - fixed + turn * (used - fixed)) % max(1, number_of - fixed)
        return jnp.zeros((number_of,), jnp.int32).at[sequence[jnp.where(places < fixed, places, shifted)]].set(jnp.asarray(sizes, jnp.int32))

    sizes = jnp.where(number % 4 == 0, named(heavy_load, number // 4), named(common, number - number // 4 - 1))
    mixed = jax.random.permutation(jax.random.fold_in(own, 3), number_of)
    donor, taker = mixed[0:number_of // 2 * 2:2], mixed[1:number_of // 2 * 2:2]
    room = jnp.minimum(sizes[donor] - 1, bound - sizes[taker]) // 2
    room = jnp.where((donor == sequence[0]) | (taker == sequence[0]) | (sizes[taker] == 0), 0, jnp.maximum(room, 0))
    shifted = jax.random.randint(jax.random.fold_in(own, 4), (number_of // 2,), 0, 1 << 20) % (room + 1)
    sizes = sizes.at[donor].add(-shifted).at[taker].add(shifted)
    members = jnp.searchsorted(jnp.cumsum(sizes), jnp.arange(rows * top), side="right").astype(jnp.int32)
    listing = members.reshape(top, rows).T
    listing = listing[jax.random.permutation(jax.random.fold_in(own, 1), rows)]
    turn = jax.random.randint(jax.random.fold_in(own, 2), (rows, 1), 0, top)
    return jnp.take_along_axis(listing, (jnp.arange(top)[None, :] + turn) % top, axis=1)


def shares(amount, total, bound, skew, full):
    loads = [(1 << 20) // math.isqrt(rank ** skew) + 1 for rank in range(1, amount + 1)]
    largest = bound if full else min(bound, max(-(-total // amount), total * loads[0] // sum(loads)))
    least = 1 if total - largest >= amount - 1 else 0
    holding, surplus = [largest] + [least] * (amount - 1), total - largest - least * (amount - 1)
    while surplus > 0:
        free = [i for i in range(1, amount) if holding[i] < largest] or [i for i in range(1, amount) if holding[i] < bound]
        pool, left = sum([loads[i] for i in free]), surplus
        for i in free:
            addition = min(bound - holding[i], max(1, left * loads[i] // pool), surplus)
            holding[i] = holding[i] + addition
            surplus = surplus - addition
    return np.array(holding)


def centred(own_key, dims, deviation, limit, split=(), held_as=jnp.bfloat16):
    result = jax.random.normal(own_key, dims, jnp.float32) * deviation
    if len(split) > 0:
        result = level_of(own_key, dims, split, -0.22, 0.18) * result
    return jnp.clip(result, min=-limit, max=limit).astype(held_as)


def setup_inputs(seed: int = 0) -> dict:
    key_list = jax.random.split(jax.random.key(seed), 7)
    latent = centred(key_list[0], (TOKENS, L), 1.0, 6.0, ((0, 32),))
    cotangent = centred(key_list[1], (TOKENS, L), 0.1, 0.59765625, ((0, 32),))
    routes_keys = jax.random.split(jax.random.fold_in(key_list[2], 1), TOKENS // T_DEV)
    routes_turns = jax.random.permutation(jax.random.fold_in(key_list[2], 3), TOKENS // T_DEV)
    routes = jax.vmap(lambda own, number: assign_block(jax.random.fold_in(key_list[2], 2), own, number, T_DEV, EXPERTS, TOP, CAP, 2))(routes_keys, routes_turns).reshape((TOKENS, TOP))
    gates = jnp.clip(jnp.exp(math.log(1.0) - 2.3025851 * jax.random.uniform(key_list[3], (TOKENS, TOP), jnp.float32) ** level_of(key_list[3], (TOKENS, TOP), ((0, 32),), -0.2, 0.2)), 0.1, 1.0)
    w_in = centred(key_list[4], (EXPERTS, L, 2 * H), L ** -0.5, 0.1875, ((0, 8),))
    w_out = centred(key_list[5], (EXPERTS, L, H), H ** -0.5, 0.1875, ((0, 8),))
    return dict(latent=latent, cotangent=cotangent, routes=routes, gates=gates, w_in=w_in, w_out=w_out)


def expert_pass(x_buf, dy_buf, w_in_e, w_out_e):
    acts = jnp.dot(x_buf, w_in_e, preferred_element_type=jnp.float32)
    gate = acts[:, :H]
    upper = acts[:, H:]
    sig = jax.nn.sigmoid(gate)
    swish = gate * sig
    hidden = (swish * upper).astype(jnp.bfloat16)
    y_buf = lax.dot_general(hidden, w_out_e, (((1,), (1,)), ((), ())), preferred_element_type=jnp.float32).astype(jnp.bfloat16)
    d_hidden = jnp.dot(dy_buf, w_out_e, preferred_element_type=jnp.float32)
    d_gate = d_hidden * upper * sig * (1.0 + gate * (1.0 - sig))
    d_upper = d_hidden * swish
    d_acts = jnp.concatenate([d_gate, d_upper], axis=1).astype(jnp.bfloat16)
    xs = x_buf.reshape(N_DP, -1, L).astype(jnp.float32)
    das = d_acts.reshape(N_DP, -1, 2 * H).astype(jnp.float32)
    dys = dy_buf.reshape(N_DP, -1, L).astype(jnp.float32)
    hids = hidden.reshape(N_DP, -1, H).astype(jnp.float32)
    part_in = jnp.einsum("drl,drk->dlk", xs, das).astype(jnp.bfloat16).astype(jnp.float32)
    part_out = jnp.einsum("drl,drk->dlk", dys, hids).astype(jnp.bfloat16).astype(jnp.float32)
    return y_buf, jnp.sum(part_in, axis=0), jnp.sum(part_out, axis=0)


def reference(latent, cotangent, routes, gates, w_in, w_out):
    blocks = N_DP * N_EXPERT
    flat = routes.reshape(blocks, T_DEV * TOP)
    onehot = (flat[:, :, None] == jnp.arange(EXPERTS, dtype=jnp.int32)[None, None, :]).astype(jnp.int32)
    before = jnp.cumsum(onehot, axis=1) - onehot
    slot = jnp.sum(before * onehot, axis=2)
    position = (jnp.arange(blocks, dtype=jnp.int32)[:, None] * CAP + slot).reshape(-1)
    route_flat = routes.reshape(-1)
    gate_flat = gates.reshape(-1)
    x_rows = jnp.repeat(latent, TOP, axis=0)
    dy_rows = (gate_flat[:, None] * jnp.repeat(cotangent, TOP, axis=0).astype(jnp.float32)).astype(jnp.bfloat16)
    size = blocks * CAP

    def one_expert(expert_id):
        index = jnp.where(route_flat == expert_id, position, size).astype(jnp.int32)
        x_buf = jnp.zeros((size, L), jnp.bfloat16).at[index].set(x_rows, mode="drop")
        dy_buf = jnp.zeros((size, L), jnp.bfloat16).at[index].set(dy_rows, mode="drop")
        return expert_pass(x_buf, dy_buf, w_in[expert_id], w_out[expert_id])

    y_bufs, grad_in, grad_out = lax.map(one_expert, jnp.arange(EXPERTS, dtype=jnp.int32))
    y_rows = y_bufs[route_flat, position].astype(jnp.float32)
    output = jnp.sum((gate_flat[:, None] * y_rows).reshape(-1, TOP, L), axis=1).astype(jnp.bfloat16)
    return output, grad_in, grad_out
```

```python
import functools

import jax
import jax.numpy as jnp
from jax import lax
from jax.experimental import pallas as pl
from jax.experimental.pallas import tpu as pltpu
from jax.sharding import PartitionSpec as P

MESH = pl.DeviceIdType.MESH
TILE = 256


def fused_kernel(
    n_exp, cap,
    lat_ref, cot_ref, routes_ref, gates_ref, win_hbm, wout_hbm,
    out_ref, gin_ref, gout_ref,
    win, wout, sx, sdy, xall, dyall, a1, a2, hid, ybuf, back, place,
    w_sem, zsend, zrecv, gsend, grecv,
):
    p = lax.axis_index("dp")
    q = lax.axis_index("expert")
    px, py = lax.rem(p, 2), lax.div(p, 2)
    xn = (py * 2 + 1 - px, q)
    yn = ((1 - py) * 2 + px, q)
    tok, width = lat_ref.shape
    rows = n_exp * cap
    hidden = hid.shape[2]
    share = gin_ref.shape[0]

    def ahead(j):
        return (p, lax.rem(q + j, n_exp))

    def behind(j):
        return (p, lax.rem(q + n_exp - j, n_exp))

    barrier = pltpu.get_barrier_semaphore()
    for j in range(1, n_exp):
        pl.semaphore_signal(barrier, inc=1, device_id=ahead(j), device_id_type=MESH)
    pl.semaphore_signal(barrier, inc=1, device_id=xn, device_id_type=MESH)
    pl.semaphore_signal(barrier, inc=1, device_id=yn, device_id_type=MESH)
    w_copies = (
        pltpu.make_async_copy(win_hbm.at[0], win, w_sem.at[0]),
        pltpu.make_async_copy(wout_hbm.at[0], wout, w_sem.at[1]),
    )
    for c in w_copies:
        c.start()

    rel = lax.rem(routes_ref[...] - q + n_exp, n_exp)
    lane = lax.broadcasted_iota(jnp.int32, (tok, 128), 1)
    onehot = jnp.where(rel == lane, 1.0, 0.0)
    lower = jnp.where(
        lax.broadcasted_iota(jnp.int32, (tok, tok), 1)
        < lax.broadcasted_iota(jnp.int32, (tok, tok), 0),
        1.0,
        0.0,
    )
    before = jnp.dot(
        lower.astype(jnp.bfloat16), onehot.astype(jnp.bfloat16), preferred_element_type=jnp.float32
    )
    slot = jnp.sum(before * onehot, axis=1, keepdims=True)
    position = rel.astype(jnp.float32) * cap + slot
    place[...] = jnp.where(
        lax.broadcasted_iota(jnp.int32, (tok, rows), 1).astype(jnp.float32) == position, 1.0, 0.0
    ).astype(jnp.bfloat16)

    def placed(value):
        return lax.dot_general(
            place[...], value, (((0,), (0,)), ((), ())), preferred_element_type=jnp.float32
        ).astype(jnp.bfloat16)

    def part(j):
        return pl.ds(j * cap, cap)

    def z_copy(kind, src, dst, j, to):
        return pltpu.make_async_remote_copy(
            src_ref=src.at[part(j)],
            dst_ref=dst.at[part(j)],
            send_sem=zsend.at[kind, j],
            recv_sem=zrecv.at[kind, j],
            device_id=to,
            device_id_type=MESH,
        )

    buffers = (xall, dyall)
    z_copies = {}
    far_first = sorted(range(1, n_exp), key=lambda j: -min(j, n_exp - j))
    near_first = [0] + far_first[::-1]

    placed_x = placed(lat_ref[...])
    sx[...] = placed_x
    xall[0, 0:cap, :] = placed_x[0:cap, :]
    pl.semaphore_wait(barrier, n_exp + 1)
    for j in far_first:
        z_copies[0, j] = z_copy(0, sx, xall.at[0], j, ahead(j))
        z_copies[0, j].start()
    placed_dy = placed((gates_ref[...] * cot_ref[...].astype(jnp.float32)).astype(jnp.bfloat16))
    sdy[...] = placed_dy
    dyall[0, 0:cap, :] = placed_dy[0:cap, :]
    for j in far_first:
        z_copies[1, j] = z_copy(1, sdy, dyall.at[0], j, ahead(j))
        z_copies[1, j].start()

    g_copies = {}
    received = set()

    def g_copy(kind, src, dst, j, to):
        c = pltpu.make_async_remote_copy(
            src_ref=buffers[kind].at[src, part(j)],
            dst_ref=buffers[kind].at[dst, part(j)],
            send_sem=gsend.at[kind, dst - 1, j],
            recv_sem=grecv.at[kind, dst - 1, j],
            device_id=to,
            device_id_type=MESH,
        )
        g_copies[kind, dst, j] = c
        c.start()

    def take(kind, group, j):
        if (kind, group, j) not in received:
            received.add((kind, group, j))
            g_copies[kind, group, j].wait_recv()

    def spread(kind, j):
        if j:
            z_copies[kind, j].wait_recv()
        g_copy(kind, 0, 1, j, xn)
        g_copy(kind, 0, 2, j, yn)

    def relay(kind, i):
        j = near_first[i]
        if i % 2 == 0:
            take(kind, 1, j)
            g_copy(kind, 1, 3, j, yn)
        else:
            take(kind, 2, j)
            g_copy(kind, 2, 3, j, xn)

    def forward(r):
        if r:
            for j in near_first:
                take(0, r, j)

        @pl.loop(0, hidden // TILE)
        def _(h):
            lo = pl.ds(pl.multiple_of(h * TILE, TILE), TILE)
            hi = pl.ds(pl.multiple_of(hidden + h * TILE, TILE), TILE)
            gate = jnp.dot(xall[r], win[:, lo], preferred_element_type=jnp.float32)
            upper = jnp.dot(xall[r], win[:, hi], preferred_element_type=jnp.float32)
            sig = jax.nn.sigmoid(gate)
            swish = gate * sig
            hid[r, :, lo] = (swish * upper).astype(jnp.bfloat16)
            a1[r, :, lo] = upper * sig * (1.0 + gate * (1.0 - sig))
            a2[r, :, lo] = swish

    def backward(r):
        if r:
            for j in near_first:
                take(1, r, j)
        cols = pl.ds(pl.multiple_of(p * share, share), share)

        @pl.loop(0, hidden // TILE)
        def _(h):
            lo = pl.ds(pl.multiple_of(h * TILE, TILE), TILE)
            hi = pl.ds(pl.multiple_of(hidden + h * TILE, TILE), TILE)
            d_hid = jnp.dot(dyall[r], wout[:, lo], preferred_element_type=jnp.float32)
            d_gate = (d_hid * a1[r, :, lo]).astype(jnp.bfloat16)
            d_upper = (d_hid * a2[r, :, lo]).astype(jnp.bfloat16)

            def add(ref, at, left, right):
                term = lax.dot_general(
                    left, right, (((0,), (0,)), ((), ())), preferred_element_type=jnp.float32
                )
                ref[:, at] = term if r == 0 else ref[:, at] + term

            add(gin_ref, lo, xall[r, :, cols], d_gate)
            add(gin_ref, hi, xall[r, :, cols], d_upper)
            add(gout_ref, lo, dyall[r, :, cols], hid[r, :, lo])

    lag = 2
    for i, j in enumerate(near_first):
        spread(0, j)
        if i >= lag:
            relay(0, i - lag)
    for c in w_copies:
        c.wait()
    forward(0)

    @pl.loop(0, width // TILE)
    def _(l):
        at = pl.ds(pl.multiple_of(l * TILE, TILE), TILE)
        ybuf[:, at] = lax.dot_general(
            hid[0], wout[at, :], (((1,), (1,)), ((), ())), preferred_element_type=jnp.float32
        ).astype(jnp.bfloat16)

    back[0:cap, :] = ybuf[0:cap, :]
    for j in far_first:
        z_copies[2, j] = z_copy(2, ybuf, back, j, behind(j))
        z_copies[2, j].start()

    for i in range(n_exp - lag, n_exp):
        relay(0, i)
    for i, j in enumerate(near_first):
        spread(1, j)
        if i >= lag:
            relay(1, i - lag)
        if i == n_exp // 2:
            forward(1)
    for i in range(n_exp - lag, n_exp):
        relay(1, i)
    forward(2)
    backward(0)
    forward(3)
    backward(1)
    backward(2)
    for j in far_first:
        z_copies[2, j].wait_recv()
    out_ref[...] = (
        gates_ref[...] * jnp.dot(place[...], back[...], preferred_element_type=jnp.float32)
    ).astype(jnp.bfloat16)
    backward(3)
    for c in z_copies.values():
        c.wait_send()
    for c in g_copies.values():
        c.wait_send()


def fused(latent, cotangent, routes, gates, w_in, w_out, n_exp, cap):
    tok, width = latent.shape
    hidden = w_out.shape[2]
    rows = n_exp * cap
    share = width // 4
    bf16, f32 = jnp.bfloat16, jnp.float32
    vmem = pl.BlockSpec(memory_space=pltpu.VMEM)
    hbm = pl.BlockSpec(memory_space=pl.ANY)
    flops = 2 * rows * width * hidden * 16
    output, grad_in, grad_out = pl.pallas_call(
        functools.partial(fused_kernel, n_exp, cap),
        out_shape=(
            jax.ShapeDtypeStruct((tok, width), bf16),
            jax.ShapeDtypeStruct((share, 2 * hidden), f32),
            jax.ShapeDtypeStruct((share, hidden), f32),
        ),
        in_specs=[vmem, vmem, vmem, vmem, hbm, hbm],
        out_specs=(vmem, vmem, vmem),
        scratch_shapes=[
            pltpu.VMEM((width, 2 * hidden), bf16),
            pltpu.VMEM((width, hidden), bf16),
            pltpu.VMEM((rows, width), bf16),
            pltpu.VMEM((rows, width), bf16),
            pltpu.VMEM((4, rows, width), bf16),
            pltpu.VMEM((4, rows, width), bf16),
            pltpu.VMEM((4, rows, hidden), f32),
            pltpu.VMEM((4, rows, hidden), f32),
            pltpu.VMEM((4, rows, hidden), bf16),
            pltpu.VMEM((rows, width), bf16),
            pltpu.VMEM((rows, width), bf16),
            pltpu.VMEM((tok, rows), bf16),
            pltpu.SemaphoreType.DMA((2,)),
            pltpu.SemaphoreType.DMA((3, n_exp)),
            pltpu.SemaphoreType.DMA((3, n_exp)),
            pltpu.SemaphoreType.DMA((2, 3, n_exp)),
            pltpu.SemaphoreType.DMA((2, 3, n_exp)),
        ],
        compiler_params=pltpu.CompilerParams(
            collective_id=0, has_side_effects=True, vmem_limit_bytes=48 * 1024 * 1024
        ),
        cost_estimate=pl.CostEstimate(
            flops=flops, bytes_accessed=10 * 1024 * 1024, transcendentals=4 * rows * hidden
        ),
    )(latent, cotangent, routes, gates, w_in, w_out)
    return output, grad_in.reshape(1, share, 2 * hidden), grad_out.reshape(1, share, hidden)


def on_device(latent, cotangent, routes, gates, w_in, w_out):
    n_experts = lax.axis_size("expert")
    n_replicas = lax.axis_size("dp")
    tok_count = latent.shape[0]
    top_count = routes.shape[1]
    width = latent.shape[1]
    hidden_units = w_out.shape[2]
    capacity = max(2, 2 * tok_count * top_count // n_experts)
    if n_replicas == 4 and top_count == 1 and capacity % 16 == 0 and tok_count == 128:
        return fused(latent, cotangent, routes, gates, w_in, w_out, n_experts, capacity)
    route_flat = routes.reshape(-1)
    gate_flat = gates.reshape(-1)
    onehot = (route_flat[:, None] == jnp.arange(n_experts, dtype=jnp.int32)[None, :]).astype(
        jnp.int32
    )
    before = jnp.cumsum(onehot, axis=0) - onehot
    slot = jnp.sum(before * onehot, axis=1)
    position = route_flat * capacity + slot
    placing = (
        jnp.arange(n_experts * capacity, dtype=jnp.int32)[:, None] == position[None, :]
    ).astype(jnp.bfloat16)
    x_rows = jnp.repeat(latent, top_count, axis=0)
    dy_rows = (
        gate_flat[:, None] * jnp.repeat(cotangent, top_count, axis=0).astype(jnp.float32)
    ).astype(jnp.bfloat16)
    send_x = (
        jnp.dot(placing, x_rows, preferred_element_type=jnp.float32)
        .astype(jnp.bfloat16)
        .reshape(n_experts, capacity, width)
    )
    send_dy = (
        jnp.dot(placing, dy_rows, preferred_element_type=jnp.float32)
        .astype(jnp.bfloat16)
        .reshape(n_experts, capacity, width)
    )
    got_x = lax.all_to_all(send_x, "expert", split_axis=0, concat_axis=0, tiled=True)
    got_dy = None
    x_buf = got_x.reshape(-1, width)
    acts = jnp.dot(x_buf, w_in[0], preferred_element_type=jnp.float32)
    gate = acts[:, :hidden_units]
    upper = acts[:, hidden_units:]
    sig = jax.nn.sigmoid(gate)
    swish = gate * sig
    hidden = (swish * upper).astype(jnp.bfloat16)
    y_buf = lax.dot_general(
        hidden, w_out[0], (((1,), (1,)), ((), ())), preferred_element_type=jnp.float32
    ).astype(jnp.bfloat16)
    back = lax.all_to_all(
        y_buf.reshape(n_experts, capacity, width), "expert", split_axis=0, concat_axis=0, tiled=True
    ).reshape(-1, width)
    y_rows = lax.dot_general(
        placing, back, (((0,), (0,)), ((), ())), preferred_element_type=jnp.float32
    )
    output = jnp.sum(
        (gate_flat[:, None] * y_rows).reshape(tok_count, top_count, width), axis=1
    ).astype(jnp.bfloat16)
    got_dy = lax.all_to_all(send_dy, "expert", split_axis=0, concat_axis=0, tiled=True)
    dy_buf = got_dy.reshape(-1, width)
    d_hidden = jnp.dot(dy_buf, w_out[0], preferred_element_type=jnp.float32)
    d_gate = d_hidden * upper * sig * (1.0 + gate * (1.0 - sig))
    d_upper = d_hidden * swish
    d_acts = jnp.concatenate([d_gate, d_upper], axis=1).astype(jnp.bfloat16)
    share = width // n_replicas
    columns = x_buf
    grad_in = lax.psum_scatter(
        lax.dot_general(
            columns, d_acts, (((0,), (0,)), ((), ())), preferred_element_type=jnp.float32
        ).astype(jnp.bfloat16),
        "dp",
        scatter_dimension=0,
        tiled=True,
    ).astype(jnp.float32)
    columns = dy_buf
    grad_out = lax.psum_scatter(
        lax.dot_general(
            columns, hidden, (((0,), (0,)), ((), ())), preferred_element_type=jnp.float32
        ).astype(jnp.bfloat16),
        "dp",
        scatter_dimension=0,
        tiled=True,
    ).astype(jnp.float32)
    return (
        output,
        grad_in.reshape(1, share, 2 * hidden_units),
        grad_out.reshape(1, share, hidden_units),
    )


def solution(mesh):
    in_specs = (
        P(("dp", "expert"), None),
        P(("dp", "expert"), None),
        P(("dp", "expert"), None),
        P(("dp", "expert"), None),
        P("expert", None, None),
        P("expert", None, None),
    )
    out_specs = (P(("dp", "expert"), None), P("expert", "dp", None), P("expert", "dp", None))
    return jax.shard_map(
        on_device, mesh=mesh, in_specs=in_specs, out_specs=out_specs, check_vma=False
    )
```

```python
import functools

import jax
import jax.numpy as jnp
from jax import lax
from jax.experimental import pallas as pl
from jax.experimental.pallas import tpu as pltpu
from jax.sharding import PartitionSpec as P

MESH = pl.DeviceIdType.MESH
TILE = 256


def fused_kernel(
    n_exp, cap,
    lat_hbm, cot_hbm, routes_ref, gates_ref, win_hbm, wout_hbm,
    out_ref, gin_ref, gout_ref,
    lat, cot, win, wout, sx, sdy, xall, dyall, a1, a2, hid, ybuf, back, place,
    in_sem, zsend, zrecv, gsend, grecv,
):
    p = lax.axis_index("dp")
    q = lax.axis_index("expert")
    px, py = lax.rem(p, 2), lax.div(p, 2)
    xn = (py * 2 + 1 - px, q)
    yn = ((1 - py) * 2 + px, q)
    tok, width = lat.shape
    rows = n_exp * cap
    hidden = hid.shape[2]
    share = gin_ref.shape[0]
    half = n_exp // 2
    order = sorted(range(n_exp), key=lambda j: (min(j, n_exp - j), j))
    far_first = list(range(1, n_exp))[::-1]

    def ahead(i):
        return (p, lax.rem(q + order[i], n_exp))

    def behind(i):
        return (p, lax.rem(q + n_exp - order[i], n_exp))

    barrier = pltpu.get_barrier_semaphore()
    for i in range(1, n_exp):
        pl.semaphore_signal(barrier, inc=1, device_id=ahead(i), device_id_type=MESH)
    pl.semaphore_signal(barrier, inc=1, device_id=xn, device_id_type=MESH)
    pl.semaphore_signal(barrier, inc=1, device_id=yn, device_id_type=MESH)
    loads = [
        pltpu.make_async_copy(src, dst, in_sem.at[n])
        for n, (src, dst) in enumerate(
            ((lat_hbm, lat), (cot_hbm, cot), (win_hbm.at[0], win), (wout_hbm.at[0], wout))
        )
    ]
    for c in loads:
        c.start()

    rel = lax.rem(routes_ref[...] - q + n_exp, n_exp)
    index = jnp.zeros_like(rel)
    for i, j in enumerate(order):
        index = jnp.where(rel == j, i, index)
    i0 = lax.broadcasted_iota(jnp.int32, (tok, tok), 0)
    i1 = lax.broadcasted_iota(jnp.int32, (tok, tok), 1)
    onehot = jnp.where(i0 == index, 1.0, 0.0)
    earlier = jnp.where(i0 < i1, 1.0, 0.0)
    before = jnp.dot(
        onehot.astype(jnp.bfloat16), earlier.astype(jnp.bfloat16), preferred_element_type=jnp.float32
    )
    slot = jnp.sum(before * onehot, axis=0, keepdims=True)
    position = index.astype(jnp.float32) * cap + slot
    place[...] = jnp.where(
        lax.broadcasted_iota(jnp.int32, (rows, tok), 0).astype(jnp.float32) == position, 1.0, 0.0
    ).astype(jnp.bfloat16)
    gates = jnp.sum(jnp.where(i0 == i1, gates_ref[...], 0.0), axis=1, keepdims=True)

    def place_rows(value, sent, kept):
        placed = jnp.dot(place[...], value, preferred_element_type=jnp.float32).astype(jnp.bfloat16)
        sent[...] = placed
        kept[0, 0:cap, :] = placed[0:cap, :]

    def at(buf, group, i):
        return buf.at[(i // half) * 2 + group // 2, pl.ds((group % 2) * (rows // 2) + (i % half) * cap, cap)]

    def slots(i):
        return pl.ds(i * cap, cap)

    def z_copy(kind, src, dst, i, to):
        c = pltpu.make_async_remote_copy(
            src_ref=src.at[slots(i)],
            dst_ref=dst,
            send_sem=zsend.at[kind, i],
            recv_sem=zrecv.at[kind, i],
            device_id=to,
            device_id_type=MESH,
        )
        z_copies[kind, i] = c
        c.start()

    buffers = (xall, dyall)
    z_copies, g_copies = {}, {}
    received = set()

    loads[0].wait()
    place_rows(lat[...], sx, xall)
    pl.semaphore_wait(barrier, n_exp + 1)
    for i in far_first:
        z_copy(0, sx, at(xall, 0, i), i, ahead(i))

    def g_copy(kind, src, dst, i, to):
        c = pltpu.make_async_remote_copy(
            src_ref=at(buffers[kind], src, i),
            dst_ref=at(buffers[kind], dst, i),
            send_sem=gsend.at[kind, dst - 1, i],
            recv_sem=grecv.at[kind, dst - 1, i],
            device_id=to,
            device_id_type=MESH,
        )
        g_copies[kind, dst, i] = c
        c.start()

    def take(kind, group, i):
        if (kind, group, i) not in received:
            received.add((kind, group, i))
            if group:
                g_copies[kind, group, i].wait_recv()
            elif i:
                z_copies[kind, i].wait_recv()

    def spread(kind, i):
        take(kind, 0, i)
        g_copy(kind, 0, 1, i, xn)
        g_copy(kind, 0, 2, i, yn)

    def relay(kind, i):
        if i % 2 == 0:
            take(kind, 1, i)
            g_copy(kind, 1, 3, i, yn)
        else:
            take(kind, 2, i)
            g_copy(kind, 2, 3, i, xn)

    def take_chunk(kind, c):
        for i in range(half):
            take(kind, c % 2 * 2, c // 2 * half + i)
            take(kind, c % 2 * 2 + 1, c // 2 * half + i)

    def forward(c):
        take_chunk(0, c)

        @pl.loop(0, hidden // TILE)
        def _(h):
            lo = pl.ds(pl.multiple_of(h * TILE, TILE), TILE)
            hi = pl.ds(pl.multiple_of(hidden + h * TILE, TILE), TILE)
            gate = jnp.dot(xall[c], win[:, lo], preferred_element_type=jnp.float32)
            upper = jnp.dot(xall[c], win[:, hi], preferred_element_type=jnp.float32)
            sig = jax.nn.sigmoid(gate)
            swish = gate * sig
            hid[c, :, lo] = (swish * upper).astype(jnp.bfloat16)
            a1[c, :, lo] = upper * sig * (1.0 + gate * (1.0 - sig))
            a2[c, :, lo] = swish

    def backward(c):
        take_chunk(1, c)
        cols = pl.ds(pl.multiple_of(p * share, share), share)

        @pl.loop(0, hidden // TILE)
        def _(h):
            lo = pl.ds(pl.multiple_of(h * TILE, TILE), TILE)
            hi = pl.ds(pl.multiple_of(hidden + h * TILE, TILE), TILE)
            d_hid = jnp.dot(dyall[c], wout[:, lo], preferred_element_type=jnp.float32)
            d_gate = (d_hid * a1[c, :, lo]).astype(jnp.bfloat16)
            d_upper = (d_hid * a2[c, :, lo]).astype(jnp.bfloat16)

            def add(ref, where, left, right):
                term = lax.dot_general(
                    left, right, (((0,), (0,)), ((), ())), preferred_element_type=jnp.float32
                )
                ref[:, where] = term if c == 0 else ref[:, where] + term

            add(gin_ref, lo, xall[c, :, cols], d_gate)
            add(gin_ref, hi, xall[c, :, cols], d_upper)
            add(gout_ref, lo, dyall[c, :, cols], hid[c, :, lo])

    def expert_out():
        @pl.loop(0, width // TILE)
        def _(l):
            tile = pl.ds(pl.multiple_of(l * TILE, TILE), TILE)
            own = jnp.concatenate([hid[0, 0 : rows // 2, :], hid[2, 0 : rows // 2, :]], axis=0)
            ybuf[:, tile] = lax.dot_general(
                own, wout[tile, :], (((1,), (1,)), ((), ())), preferred_element_type=jnp.float32
            ).astype(jnp.bfloat16)

        back[0:cap, :] = ybuf[0:cap, :]

    spread(0, 0)
    loads[1].wait()
    place_rows((gates * cot[...].astype(jnp.float32)).astype(jnp.bfloat16), sdy, dyall)
    for i in range(1, n_exp):
        spread(0, i)
        k = far_first[i - 1]
        z_copy(1, sdy, at(dyall, 0, k), k, ahead(k))
        if i >= 2:
            relay(0, i - 2)
    spread(1, 0)
    spread(1, 1)
    loads[2].wait()
    loads[3].wait()
    forward(0)
    relay(0, n_exp - 2)
    relay(0, n_exp - 1)
    spread(1, 2)
    relay(1, 0)
    forward(2)
    expert_out()
    spread(1, 3)
    relay(1, 1)
    for i in far_first:
        z_copy(2, ybuf, back.at[slots(i)], i, behind(i))
    forward(1)
    spread(1, 4)
    relay(1, 2)
    forward(3)
    spread(1, 5)
    relay(1, 3)
    backward(0)
    spread(1, 6)
    relay(1, 4)
    spread(1, 7)
    relay(1, 5)
    backward(1)
    relay(1, 6)
    relay(1, 7)
    backward(2)
    for i in far_first:
        z_copies[2, i].wait_recv()
    out_ref[...] = (
        gates
        * lax.dot_general(
            place[...], back[...], (((0,), (0,)), ((), ())), preferred_element_type=jnp.float32
        )
    ).astype(jnp.bfloat16)
    backward(3)
    for c in z_copies.values():
        c.wait_send()
    for c in g_copies.values():
        c.wait_send()


def store_kernel(*refs):
    count = len(refs) // 2
    copies = [
        pltpu.make_async_copy(refs[n], refs[count + n], refs[-1].at[n]) for n in range(count)
    ]
    for c in copies:
        c.start()
    for c in copies:
        c.wait()


def fused(latent, cotangent, routes, gates, w_in, w_out, n_exp, cap):
    tok, width = latent.shape
    hidden = w_out.shape[2]
    rows = n_exp * cap
    share = width // 4
    bf16, f32 = jnp.bfloat16, jnp.float32
    vmem = pl.BlockSpec(memory_space=pltpu.VMEM)
    hbm = pl.BlockSpec(memory_space=pltpu.HBM)
    anywhere = pl.BlockSpec(memory_space=pl.ANY)
    flops = 2 * rows * width * hidden * 16
    shapes = (
        jax.ShapeDtypeStruct((tok, width), bf16),
        jax.ShapeDtypeStruct((share, 2 * hidden), f32),
        jax.ShapeDtypeStruct((share, hidden), f32),
    )
    results = pl.pallas_call(
        functools.partial(fused_kernel, n_exp, cap),
        out_shape=shapes,
        in_specs=[hbm, hbm, vmem, vmem, hbm, hbm],
        out_specs=(vmem, vmem, vmem),
        scratch_shapes=[
            pltpu.VMEM((tok, width), bf16),
            pltpu.VMEM((tok, width), bf16),
            pltpu.VMEM((width, 2 * hidden), bf16),
            pltpu.VMEM((width, hidden), bf16),
            pltpu.VMEM((rows, width), bf16),
            pltpu.VMEM((rows, width), bf16),
            pltpu.VMEM((4, rows, width), bf16),
            pltpu.VMEM((4, rows, width), bf16),
            pltpu.VMEM((4, rows, hidden), f32),
            pltpu.VMEM((4, rows, hidden), f32),
            pltpu.VMEM((4, rows, hidden), bf16),
            pltpu.VMEM((rows, width), bf16),
            pltpu.VMEM((rows, width), bf16),
            pltpu.VMEM((rows, tok), bf16),
            pltpu.SemaphoreType.DMA((4,)),
            pltpu.SemaphoreType.DMA((3, n_exp)),
            pltpu.SemaphoreType.DMA((3, n_exp)),
            pltpu.SemaphoreType.DMA((2, 3, n_exp)),
            pltpu.SemaphoreType.DMA((2, 3, n_exp)),
        ],
        compiler_params=pltpu.CompilerParams(
            collective_id=0, has_side_effects=True, vmem_limit_bytes=48 * 1024 * 1024
        ),
        cost_estimate=pl.CostEstimate(
            flops=flops, bytes_accessed=10 * 1024 * 1024, transcendentals=4 * rows * hidden
        ),
    )(latent, cotangent, routes.reshape(1, tok), gates.reshape(1, tok), w_in, w_out)
    output, grad_in, grad_out = pl.pallas_call(
        store_kernel,
        out_shape=shapes,
        in_specs=[anywhere] * 3,
        out_specs=(hbm, hbm, hbm),
        scratch_shapes=[pltpu.SemaphoreType.DMA((3,))],
        cost_estimate=pl.CostEstimate(flops=0, bytes_accessed=7 * 1024 * 1024, transcendentals=0),
    )(*results)
    return output, grad_in.reshape(1, share, 2 * hidden), grad_out.reshape(1, share, hidden)


def on_device(latent, cotangent, routes, gates, w_in, w_out):
    n_experts = lax.axis_size("expert")
    n_replicas = lax.axis_size("dp")
    tok_count = latent.shape[0]
    top_count = routes.shape[1]
    width = latent.shape[1]
    hidden_units = w_out.shape[2]
    capacity = max(2, 2 * tok_count * top_count // n_experts)
    if n_replicas == 4 and top_count == 1 and capacity % 16 == 0 and tok_count == 128 and n_experts == 8:
        return fused(latent, cotangent, routes, gates, w_in, w_out, n_experts, capacity)
    route_flat = routes.reshape(-1)
    gate_flat = gates.reshape(-1)
    onehot = (route_flat[:, None] == jnp.arange(n_experts, dtype=jnp.int32)[None, :]).astype(
        jnp.int32
    )
    before = jnp.cumsum(onehot, axis=0) - onehot
    slot = jnp.sum(before * onehot, axis=1)
    position = route_flat * capacity + slot
    placing = (
        jnp.arange(n_experts * capacity, dtype=jnp.int32)[:, None] == position[None, :]
    ).astype(jnp.bfloat16)
    x_rows = jnp.repeat(latent, top_count, axis=0)
    dy_rows = (
        gate_flat[:, None] * jnp.repeat(cotangent, top_count, axis=0).astype(jnp.float32)
    ).astype(jnp.bfloat16)
    send_x = (
        jnp.dot(placing, x_rows, preferred_element_type=jnp.float32)
        .astype(jnp.bfloat16)
        .reshape(n_experts, capacity, width)
    )
    send_dy = (
        jnp.dot(placing, dy_rows, preferred_element_type=jnp.float32)
        .astype(jnp.bfloat16)
        .reshape(n_experts, capacity, width)
    )
    got_x = lax.all_to_all(send_x, "expert", split_axis=0, concat_axis=0, tiled=True)
    got_dy = None
    x_buf = got_x.reshape(-1, width)
    acts = jnp.dot(x_buf, w_in[0], preferred_element_type=jnp.float32)
    gate = acts[:, :hidden_units]
    upper = acts[:, hidden_units:]
    sig = jax.nn.sigmoid(gate)
    swish = gate * sig
    hidden = (swish * upper).astype(jnp.bfloat16)
    y_buf = lax.dot_general(
        hidden, w_out[0], (((1,), (1,)), ((), ())), preferred_element_type=jnp.float32
    ).astype(jnp.bfloat16)
    back = lax.all_to_all(
        y_buf.reshape(n_experts, capacity, width), "expert", split_axis=0, concat_axis=0, tiled=True
    ).reshape(-1, width)
    y_rows = lax.dot_general(
        placing, back, (((0,), (0,)), ((), ())), preferred_element_type=jnp.float32
    )
    output = jnp.sum(
        (gate_flat[:, None] * y_rows).reshape(tok_count, top_count, width), axis=1
    ).astype(jnp.bfloat16)
    got_dy = lax.all_to_all(send_dy, "expert", split_axis=0, concat_axis=0, tiled=True)
    dy_buf = got_dy.reshape(-1, width)
    d_hidden = jnp.dot(dy_buf, w_out[0], preferred_element_type=jnp.float32)
    d_gate = d_hidden * upper * sig * (1.0 + gate * (1.0 - sig))
    d_upper = d_hidden * swish
    d_acts = jnp.concatenate([d_gate, d_upper], axis=1).astype(jnp.bfloat16)
    share = width // n_replicas
    columns = x_buf
    grad_in = lax.psum_scatter(
        lax.dot_general(
            columns, d_acts, (((0,), (0,)), ((), ())), preferred_element_type=jnp.float32
        ).astype(jnp.bfloat16),
        "dp",
        scatter_dimension=0,
        tiled=True,
    ).astype(jnp.float32)
    columns = dy_buf
    grad_out = lax.psum_scatter(
        lax.dot_general(
            columns, hidden, (((0,), (0,)), ((), ())), preferred_element_type=jnp.float32
        ).astype(jnp.bfloat16),
        "dp",
        scatter_dimension=0,
        tiled=True,
    ).astype(jnp.float32)
    return (
        output,
        grad_in.reshape(1, share, 2 * hidden_units),
        grad_out.reshape(1, share, hidden_units),
    )


def solution(mesh):
    in_specs = (
        P(("dp", "expert"), None),
        P(("dp", "expert"), None),
        P(("dp", "expert"), None),
        P(("dp", "expert"), None),
        P("expert", None, None),
        P("expert", None, None),
    )
    out_specs = (P(("dp", "expert"), None), P("expert", "dp", None), P("expert", "dp", None))
    return jax.shard_map(
        on_device, mesh=mesh, in_specs=in_specs, out_specs=out_specs, check_vma=False
    )
```

```python
import functools

import jax
import jax.numpy as jnp
from jax import lax
from jax.experimental import pallas as pl
from jax.experimental.pallas import tpu as pltpu
from jax.sharding import PartitionSpec as P

MESH = pl.DeviceIdType.MESH
TILE = 256


def fused_kernel(
    n_exp, cap,
    lat_hbm, cot_hbm, routes_ref, gates_ref, win_hbm, wout_hbm,
    out_hbm, gin_hbm, gout_hbm,
    out, gin, gout, lat, cot, win, wout, sx, sdy, xall, dyall, a1, a2, hid, ybuf, back, place,
    in_sem, out_sem, zsend, zrecv, gsend, grecv,
):
    p = lax.axis_index("dp")
    q = lax.axis_index("expert")
    px, py = lax.rem(p, 2), lax.div(p, 2)
    xn = (py * 2 + 1 - px, q)
    yn = ((1 - py) * 2 + px, q)
    tok, width = lat.shape
    rows = n_exp * cap
    hidden = hid.shape[2]
    share = gin.shape[0]
    half = n_exp // 2
    order = sorted(range(n_exp), key=lambda j: (min(j, n_exp - j), j))
    far_first = list(range(1, n_exp))[::-1]

    def ahead(i):
        return (p, lax.rem(q + order[i], n_exp))

    def behind(i):
        return (p, lax.rem(q + n_exp - order[i], n_exp))

    barrier = pltpu.get_barrier_semaphore()
    for i in range(1, n_exp):
        pl.semaphore_signal(barrier, inc=1, device_id=ahead(i), device_id_type=MESH)
    pl.semaphore_signal(barrier, inc=1, device_id=xn, device_id_type=MESH)
    pl.semaphore_signal(barrier, inc=1, device_id=yn, device_id_type=MESH)
    loads = [
        pltpu.make_async_copy(src, dst, in_sem.at[n])
        for n, (src, dst) in enumerate(
            ((lat_hbm, lat), (cot_hbm, cot), (win_hbm.at[0], win), (wout_hbm.at[0], wout))
        )
    ]
    for c in loads:
        c.start()

    rel = lax.rem(routes_ref[...] - q + n_exp, n_exp)
    index = jnp.zeros_like(rel)
    for i, j in enumerate(order):
        index = jnp.where(rel == j, i, index)
    i0 = lax.broadcasted_iota(jnp.int32, (tok, tok), 0)
    i1 = lax.broadcasted_iota(jnp.int32, (tok, tok), 1)
    onehot = jnp.where(i0 == index, 1.0, 0.0)
    earlier = jnp.where(i0 < i1, 1.0, 0.0)
    before = jnp.dot(
        onehot.astype(jnp.bfloat16), earlier.astype(jnp.bfloat16), preferred_element_type=jnp.float32
    )
    slot = jnp.sum(before * onehot, axis=0, keepdims=True)
    position = index.astype(jnp.float32) * cap + slot
    place[...] = jnp.where(
        lax.broadcasted_iota(jnp.int32, (rows, tok), 0).astype(jnp.float32) == position, 1.0, 0.0
    ).astype(jnp.bfloat16)
    gates = jnp.sum(jnp.where(i0 == i1, gates_ref[...], 0.0), axis=1, keepdims=True)

    def place_rows(value, sent, kept):
        placed = jnp.dot(place[...], value, preferred_element_type=jnp.float32).astype(jnp.bfloat16)
        sent[...] = placed
        kept[0, 0:cap, :] = placed[0:cap, :]

    def at(buf, group, i):
        if group in (0, 3):
            return buf.at[group, pl.ds(i * cap, cap)]
        return buf.at[1 + i // half, pl.ds((group - 1) * (rows // 2) + (i % half) * cap, cap)]

    def slots(i):
        return pl.ds(i * cap, cap)

    def z_copy(kind, src, dst, i, to):
        c = pltpu.make_async_remote_copy(
            src_ref=src.at[slots(i)],
            dst_ref=dst,
            send_sem=zsend.at[kind, i],
            recv_sem=zrecv.at[kind, i],
            device_id=to,
            device_id_type=MESH,
        )
        z_copies[kind, i] = c
        c.start()

    buffers = (xall, dyall)
    z_copies, g_copies = {}, {}
    received = set()

    loads[0].wait()
    place_rows(lat[...], sx, xall)
    pl.semaphore_wait(barrier, n_exp + 1)
    for i in far_first:
        z_copy(0, sx, at(xall, 0, i), i, ahead(i))

    def g_copy(kind, src, dst, i, to):
        c = pltpu.make_async_remote_copy(
            src_ref=at(buffers[kind], src, i),
            dst_ref=at(buffers[kind], dst, i),
            send_sem=gsend.at[kind, dst - 1, i],
            recv_sem=grecv.at[kind, dst - 1, i],
            device_id=to,
            device_id_type=MESH,
        )
        g_copies[kind, dst, i] = c
        c.start()

    def take(kind, group, i):
        if (kind, group, i) not in received:
            received.add((kind, group, i))
            if group:
                g_copies[kind, group, i].wait_recv()
            elif i:
                z_copies[kind, i].wait_recv()

    def spread(kind, i):
        take(kind, 0, i)
        g_copy(kind, 0, 1, i, xn)
        g_copy(kind, 0, 2, i, yn)

    def relay(kind, i):
        if i % 2 == 0:
            take(kind, 1, i)
            g_copy(kind, 1, 3, i, yn)
        else:
            take(kind, 2, i)
            g_copy(kind, 2, 3, i, xn)

    def take_chunk(kind, c):
        if c in (0, 3):
            for i in range(n_exp):
                take(kind, c, i)
        else:
            for i in range((c - 1) * half, c * half):
                take(kind, 1, i)
                take(kind, 2, i)

    def forward(c):
        take_chunk(0, c)

        @pl.loop(0, hidden // TILE)
        def _(h):
            lo = pl.ds(pl.multiple_of(h * TILE, TILE), TILE)
            hi = pl.ds(pl.multiple_of(hidden + h * TILE, TILE), TILE)
            gate = jnp.dot(xall[c], win[:, lo], preferred_element_type=jnp.float32)
            upper = jnp.dot(xall[c], win[:, hi], preferred_element_type=jnp.float32)
            sig = jax.nn.sigmoid(gate)
            swish = gate * sig
            hid[c, :, lo] = (swish * upper).astype(jnp.bfloat16)
            a1[c, :, lo] = upper * sig * (1.0 + gate * (1.0 - sig))
            a2[c, :, lo] = swish

    def backward(c):
        take_chunk(1, c)
        cols = pl.ds(pl.multiple_of(p * share, share), share)

        @pl.loop(0, hidden // TILE)
        def _(h):
            lo = pl.ds(pl.multiple_of(h * TILE, TILE), TILE)
            hi = pl.ds(pl.multiple_of(hidden + h * TILE, TILE), TILE)
            d_hid = jnp.dot(dyall[c], wout[:, lo], preferred_element_type=jnp.float32)
            d_gate = (d_hid * a1[c, :, lo]).astype(jnp.bfloat16)
            d_upper = (d_hid * a2[c, :, lo]).astype(jnp.bfloat16)

            def add(ref, where, left, right):
                term = lax.dot_general(
                    left, right, (((0,), (0,)), ((), ())), preferred_element_type=jnp.float32
                )
                ref[:, where] = term if c == 0 else ref[:, where] + term

            add(gin, lo, xall[c, :, cols], d_gate)
            add(gin, hi, xall[c, :, cols], d_upper)
            add(gout, lo, dyall[c, :, cols], hid[c, :, lo])
            if c == 3:
                for copy in stores(h):
                    copy.start()

    def stores(h):
        lo = pl.ds(pl.multiple_of(h * TILE, TILE), TILE)
        hi = pl.ds(pl.multiple_of(hidden + h * TILE, TILE), TILE)
        pairs = ((gin, gin_hbm, lo), (gin, gin_hbm, hi), (gout, gout_hbm, lo))
        return [
            pltpu.make_async_copy(src.at[:, where], dst.at[:, where], out_sem.at[n, h])
            for n, (src, dst, where) in enumerate(pairs)
        ]

    def expert_out():
        @pl.loop(0, width // TILE)
        def _(l):
            tile = pl.ds(pl.multiple_of(l * TILE, TILE), TILE)
            ybuf[:, tile] = lax.dot_general(
                hid[0], wout[tile, :], (((1,), (1,)), ((), ())), preferred_element_type=jnp.float32
            ).astype(jnp.bfloat16)

        back[0:cap, :] = ybuf[0:cap, :]

    spread(0, 0)
    loads[1].wait()
    place_rows((gates * cot[...].astype(jnp.float32)).astype(jnp.bfloat16), sdy, dyall)
    for i in range(1, n_exp):
        spread(0, i)
        k = ([1] + far_first[:-1])[i - 1]
        z_copy(1, sdy, at(dyall, 0, k), k, ahead(k))
    spread(1, 0)
    spread(1, 1)
    loads[2].wait()
    loads[3].wait()
    forward(0)
    expert_out()
    for i in far_first:
        z_copy(2, ybuf, back.at[slots(i)], i, behind(i))
    for i in range(n_exp):
        relay(0, i)
    spread(1, 2)
    spread(1, 3)
    relay(1, 0)
    forward(1)
    spread(1, 4)
    relay(1, 1)
    forward(2)
    spread(1, 5)
    relay(1, 2)
    relay(1, 3)
    forward(3)
    spread(1, 6)
    spread(1, 7)
    relay(1, 4)
    relay(1, 5)
    backward(0)
    relay(1, 6)
    relay(1, 7)
    backward(1)
    backward(2)
    for i in far_first:
        z_copies[2, i].wait_recv()
    out[...] = (
        gates
        * lax.dot_general(
            place[...], back[...], (((0,), (0,)), ((), ())), preferred_element_type=jnp.float32
        )
    ).astype(jnp.bfloat16)
    out_copy = pltpu.make_async_copy(out, out_hbm, in_sem.at[4])
    out_copy.start()
    backward(3)
    for c in z_copies.values():
        c.wait_send()
    for c in g_copies.values():
        c.wait_send()
    out_copy.wait()
    for h in range(hidden // TILE):
        for c in stores(h):
            c.wait()


def fused(latent, cotangent, routes, gates, w_in, w_out, n_exp, cap):
    tok, width = latent.shape
    hidden = w_out.shape[2]
    rows = n_exp * cap
    share = width // 4
    bf16, f32 = jnp.bfloat16, jnp.float32
    vmem = pl.BlockSpec(memory_space=pltpu.VMEM)
    hbm = pl.BlockSpec(memory_space=pltpu.HBM)
    flops = 2 * rows * width * hidden * 16
    shapes = (
        jax.ShapeDtypeStruct((tok, width), bf16),
        jax.ShapeDtypeStruct((share, 2 * hidden), f32),
        jax.ShapeDtypeStruct((share, hidden), f32),
    )
    output, grad_in, grad_out = pl.pallas_call(
        functools.partial(fused_kernel, n_exp, cap),
        out_shape=shapes,
        in_specs=[hbm, hbm, vmem, vmem, hbm, hbm],
        out_specs=(hbm, hbm, hbm),
        scratch_shapes=[
            pltpu.VMEM((tok, width), bf16),
            pltpu.VMEM((share, 2 * hidden), f32),
            pltpu.VMEM((share, hidden), f32),
            pltpu.VMEM((tok, width), bf16),
            pltpu.VMEM((tok, width), bf16),
            pltpu.VMEM((width, 2 * hidden), bf16),
            pltpu.VMEM((width, hidden), bf16),
            pltpu.VMEM((rows, width), bf16),
            pltpu.VMEM((rows, width), bf16),
            pltpu.VMEM((4, rows, width), bf16),
            pltpu.VMEM((4, rows, width), bf16),
            pltpu.VMEM((4, rows, hidden), f32),
            pltpu.VMEM((4, rows, hidden), f32),
            pltpu.VMEM((4, rows, hidden), bf16),
            pltpu.VMEM((rows, width), bf16),
            pltpu.VMEM((rows, width), bf16),
            pltpu.VMEM((rows, tok), bf16),
            pltpu.SemaphoreType.DMA((5,)),
            pltpu.SemaphoreType.DMA((3, hidden // TILE)),
            pltpu.SemaphoreType.DMA((3, n_exp)),
            pltpu.SemaphoreType.DMA((3, n_exp)),
            pltpu.SemaphoreType.DMA((2, 3, n_exp)),
            pltpu.SemaphoreType.DMA((2, 3, n_exp)),
        ],
        compiler_params=pltpu.CompilerParams(
            collective_id=0, has_side_effects=True, vmem_limit_bytes=60 * 1024 * 1024
        ),
        cost_estimate=pl.CostEstimate(
            flops=flops, bytes_accessed=10 * 1024 * 1024, transcendentals=4 * rows * hidden
        ),
    )(latent, cotangent, routes.reshape(1, tok), gates.reshape(1, tok), w_in, w_out)
    return output, grad_in.reshape(1, share, 2 * hidden), grad_out.reshape(1, share, hidden)


def on_device(latent, cotangent, routes, gates, w_in, w_out):
    n_experts = lax.axis_size("expert")
    n_replicas = lax.axis_size("dp")
    tok_count = latent.shape[0]
    top_count = routes.shape[1]
    width = latent.shape[1]
    hidden_units = w_out.shape[2]
    capacity = max(2, 2 * tok_count * top_count // n_experts)
    if n_replicas == 4 and top_count == 1 and capacity % 16 == 0 and tok_count == 128 and n_experts == 8:
        return fused(latent, cotangent, routes, gates, w_in, w_out, n_experts, capacity)
    route_flat = routes.reshape(-1)
    gate_flat = gates.reshape(-1)
    onehot = (route_flat[:, None] == jnp.arange(n_experts, dtype=jnp.int32)[None, :]).astype(
        jnp.int32
    )
    before = jnp.cumsum(onehot, axis=0) - onehot
    slot = jnp.sum(before * onehot, axis=1)
    position = route_flat * capacity + slot
    placing = (
        jnp.arange(n_experts * capacity, dtype=jnp.int32)[:, None] == position[None, :]
    ).astype(jnp.bfloat16)
    x_rows = jnp.repeat(latent, top_count, axis=0)
    dy_rows = (
        gate_flat[:, None] * jnp.repeat(cotangent, top_count, axis=0).astype(jnp.float32)
    ).astype(jnp.bfloat16)
    send_x = (
        jnp.dot(placing, x_rows, preferred_element_type=jnp.float32)
        .astype(jnp.bfloat16)
        .reshape(n_experts, capacity, width)
    )
    send_dy = (
        jnp.dot(placing, dy_rows, preferred_element_type=jnp.float32)
        .astype(jnp.bfloat16)
        .reshape(n_experts, capacity, width)
    )
    got_x = lax.all_to_all(send_x, "expert", split_axis=0, concat_axis=0, tiled=True)
    got_dy = None
    x_buf = got_x.reshape(-1, width)
    acts = jnp.dot(x_buf, w_in[0], preferred_element_type=jnp.float32)
    gate = acts[:, :hidden_units]
    upper = acts[:, hidden_units:]
    sig = jax.nn.sigmoid(gate)
    swish = gate * sig
    hidden = (swish * upper).astype(jnp.bfloat16)
    y_buf = lax.dot_general(
        hidden, w_out[0], (((1,), (1,)), ((), ())), preferred_element_type=jnp.float32
    ).astype(jnp.bfloat16)
    back = lax.all_to_all(
        y_buf.reshape(n_experts, capacity, width), "expert", split_axis=0, concat_axis=0, tiled=True
    ).reshape(-1, width)
    y_rows = lax.dot_general(
        placing, back, (((0,), (0,)), ((), ())), preferred_element_type=jnp.float32
    )
    output = jnp.sum(
        (gate_flat[:, None] * y_rows).reshape(tok_count, top_count, width), axis=1
    ).astype(jnp.bfloat16)
    got_dy = lax.all_to_all(send_dy, "expert", split_axis=0, concat_axis=0, tiled=True)
    dy_buf = got_dy.reshape(-1, width)
    d_hidden = jnp.dot(dy_buf, w_out[0], preferred_element_type=jnp.float32)
    d_gate = d_hidden * upper * sig * (1.0 + gate * (1.0 - sig))
    d_upper = d_hidden * swish
    d_acts = jnp.concatenate([d_gate, d_upper], axis=1).astype(jnp.bfloat16)
    share = width // n_replicas
    columns = x_buf
    grad_in = lax.psum_scatter(
        lax.dot_general(
            columns, d_acts, (((0,), (0,)), ((), ())), preferred_element_type=jnp.float32
        ).astype(jnp.bfloat16),
        "dp",
        scatter_dimension=0,
        tiled=True,
    ).astype(jnp.float32)
    columns = dy_buf
    grad_out = lax.psum_scatter(
        lax.dot_general(
            columns, hidden, (((0,), (0,)), ((), ())), preferred_element_type=jnp.float32
        ).astype(jnp.bfloat16),
        "dp",
        scatter_dimension=0,
        tiled=True,
    ).astype(jnp.float32)
    return (
        output,
        grad_in.reshape(1, share, 2 * hidden_units),
        grad_out.reshape(1, share, hidden_units),
    )


def solution(mesh):
    in_specs = (
        P(("dp", "expert"), None),
        P(("dp", "expert"), None),
        P(("dp", "expert"), None),
        P(("dp", "expert"), None),
        P("expert", None, None),
        P("expert", None, None),
    )
    out_specs = (P(("dp", "expert"), None), P("expert", "dp", None), P("expert", "dp", None))
    return jax.shard_map(
        on_device, mesh=mesh, in_specs=in_specs, out_specs=out_specs, check_vma=False
    )
```

```python
import functools

import jax
import jax.numpy as jnp
from jax import lax
from jax.experimental import pallas as pl
from jax.experimental.pallas import tpu as pltpu
from jax.sharding import PartitionSpec as P

MESH = pl.DeviceIdType.MESH
TILE = 256


def fused_kernel(
    n_exp, cap,
    lat_hbm, cot_hbm, routes_ref, gates_ref, win_hbm, wout_hbm,
    out_hbm, gin_hbm, gout_hbm,
    out, gin, gout, lat, cot, win, wout, sx, sdy, xall, dyall, a1, a2, hid, ybuf, back, place,
    in_sem, out_sem, zsend, zrecv, gsend, grecv,
):
    p = lax.axis_index("dp")
    q = lax.axis_index("expert")
    px, py = lax.rem(p, 2), lax.div(p, 2)
    xn = (py * 2 + 1 - px, q)
    yn = ((1 - py) * 2 + px, q)
    tok, width = lat.shape
    rows = n_exp * cap
    hidden = hid.shape[2]
    share = gin.shape[0]
    half = n_exp // 2
    z, core = lax.div(q, 2), lax.rem(q, 2)

    def partner_of(i):
        line = (z, z + 1 - 2 * lax.rem(z, 2), lax.rem(z + 2, 4), 3 - z)[i // 2]
        return line * 2 + (core if i % 2 == 0 else 1 - core)

    partners = [partner_of(i) for i in range(n_exp)]
    far_first = [4, 5, 6, 7, 2, 3, 1]

    def peer(i):
        return (p, partners[i])

    barrier = pltpu.get_barrier_semaphore()
    for i in range(1, n_exp):
        pl.semaphore_signal(barrier, inc=1, device_id=peer(i), device_id_type=MESH)
    pl.semaphore_signal(barrier, inc=1, device_id=xn, device_id_type=MESH)
    pl.semaphore_signal(barrier, inc=1, device_id=yn, device_id_type=MESH)
    loads = [
        pltpu.make_async_copy(src, dst, in_sem.at[n])
        for n, (src, dst) in enumerate(
            ((lat_hbm, lat), (cot_hbm, cot), (win_hbm.at[0], win), (wout_hbm.at[0], wout))
        )
    ]
    for c in loads:
        c.start()

    routes = routes_ref[...]
    index = jnp.zeros_like(routes)
    for i in range(1, n_exp):
        index = jnp.where(routes == partners[i], i, index)
    i0 = lax.broadcasted_iota(jnp.int32, (tok, tok), 0)
    i1 = lax.broadcasted_iota(jnp.int32, (tok, tok), 1)
    onehot = jnp.where(i0 == index, 1.0, 0.0)
    earlier = jnp.where(i0 < i1, 1.0, 0.0)
    before = jnp.dot(
        onehot.astype(jnp.bfloat16), earlier.astype(jnp.bfloat16), preferred_element_type=jnp.float32
    )
    slot = jnp.sum(before * onehot, axis=0, keepdims=True)
    position = index.astype(jnp.float32) * cap + slot
    place[...] = jnp.where(
        lax.broadcasted_iota(jnp.int32, (rows, tok), 0).astype(jnp.float32) == position, 1.0, 0.0
    ).astype(jnp.bfloat16)
    gates = jnp.sum(jnp.where(i0 == i1, gates_ref[...], 0.0), axis=1, keepdims=True)

    def place_rows(value, sent, kept):
        placed = jnp.dot(place[...], value, preferred_element_type=jnp.float32).astype(jnp.bfloat16)
        sent[...] = placed
        kept[0, 0:cap, :] = placed[0:cap, :]

    def at(buf, group, i):
        if group in (0, 3):
            return buf.at[group, pl.ds(i * cap, cap)]
        return buf.at[1 + i // half, pl.ds((group - 1) * (rows // 2) + (i % half) * cap, cap)]

    def slots(i):
        return pl.ds(i * cap, cap)

    def z_copy(kind, src, dst, i, to):
        c = pltpu.make_async_remote_copy(
            src_ref=src.at[slots(i)],
            dst_ref=dst,
            send_sem=zsend.at[kind, i],
            recv_sem=zrecv.at[kind, i],
            device_id=to,
            device_id_type=MESH,
        )
        z_copies[kind, i] = c
        c.start()

    buffers = (xall, dyall)
    z_copies, g_copies = {}, {}
    received = set()

    loads[0].wait()
    place_rows(lat[...], sx, xall)
    pl.semaphore_wait(barrier, n_exp + 1)
    for i in (1, 4, 2, 5, 3, 6, 7):
        z_copy(0, sx, at(xall, 0, i), i, peer(i))

    def g_copy(kind, src, dst, i, to):
        c = pltpu.make_async_remote_copy(
            src_ref=at(buffers[kind], src, i),
            dst_ref=at(buffers[kind], dst, i),
            send_sem=gsend.at[kind, dst - 1, i],
            recv_sem=grecv.at[kind, dst - 1, i],
            device_id=to,
            device_id_type=MESH,
        )
        g_copies[kind, dst, i] = c
        c.start()

    def take(kind, group, i):
        if (kind, group, i) not in received:
            received.add((kind, group, i))
            if group:
                g_copies[kind, group, i].wait_recv()
            elif i:
                z_copies[kind, i].wait_recv()

    def spread(kind, i):
        take(kind, 0, i)
        g_copy(kind, 0, 1, i, xn)
        g_copy(kind, 0, 2, i, yn)

    def relay(kind, i):
        if i % 2 == 0:
            take(kind, 1, i)
            g_copy(kind, 1, 3, i, yn)
        else:
            take(kind, 2, i)
            g_copy(kind, 2, 3, i, xn)

    def take_chunk(kind, c):
        if c in (0, 3):
            for i in range(n_exp):
                take(kind, c, i)
        else:
            for i in range((c - 1) * half, c * half):
                take(kind, 1, i)
                take(kind, 2, i)

    def forward(c):
        take_chunk(0, c)

        @pl.loop(0, hidden // TILE)
        def _(h):
            lo = pl.ds(pl.multiple_of(h * TILE, TILE), TILE)
            hi = pl.ds(pl.multiple_of(hidden + h * TILE, TILE), TILE)
            gate = jnp.dot(xall[c], win[:, lo], preferred_element_type=jnp.float32)
            upper = jnp.dot(xall[c], win[:, hi], preferred_element_type=jnp.float32)
            sig = jax.nn.sigmoid(gate)
            swish = gate * sig
            hid[c, :, lo] = (swish * upper).astype(jnp.bfloat16)
            a1[c, :, lo] = upper * sig * (1.0 + gate * (1.0 - sig))
            a2[c, :, lo] = swish

    def backward(c):
        take_chunk(1, c)
        cols = pl.ds(pl.multiple_of(p * share, share), share)

        @pl.loop(0, hidden // TILE)
        def _(h):
            lo = pl.ds(pl.multiple_of(h * TILE, TILE), TILE)
            hi = pl.ds(pl.multiple_of(hidden + h * TILE, TILE), TILE)
            d_hid = jnp.dot(dyall[c], wout[:, lo], preferred_element_type=jnp.float32)
            d_gate = (d_hid * a1[c, :, lo]).astype(jnp.bfloat16)
            d_upper = (d_hid * a2[c, :, lo]).astype(jnp.bfloat16)

            def add(ref, where, left, right):
                term = lax.dot_general(
                    left, right, (((0,), (0,)), ((), ())), preferred_element_type=jnp.float32
                )
                ref[:, where] = term if c == 0 else ref[:, where] + term

            add(gin, lo, xall[c, :, cols], d_gate)
            add(gin, hi, xall[c, :, cols], d_upper)
            add(gout, lo, dyall[c, :, cols], hid[c, :, lo])
            if c == 3:
                for copy in stores(h):
                    copy.start()

    def stores(h):
        lo = pl.ds(pl.multiple_of(h * TILE, TILE), TILE)
        hi = pl.ds(pl.multiple_of(hidden + h * TILE, TILE), TILE)
        pairs = ((gin, gin_hbm, lo), (gin, gin_hbm, hi), (gout, gout_hbm, lo))
        return [
            pltpu.make_async_copy(src.at[:, where], dst.at[:, where], out_sem.at[n, h])
            for n, (src, dst, where) in enumerate(pairs)
        ]

    def expert_out():
        @pl.loop(0, width // TILE)
        def _(l):
            tile = pl.ds(pl.multiple_of(l * TILE, TILE), TILE)
            ybuf[:, tile] = lax.dot_general(
                hid[0], wout[tile, :], (((1,), (1,)), ((), ())), preferred_element_type=jnp.float32
            ).astype(jnp.bfloat16)

        back[0:cap, :] = ybuf[0:cap, :]

    spread(0, 0)
    loads[1].wait()
    place_rows((gates * cot[...].astype(jnp.float32)).astype(jnp.bfloat16), sdy, dyall)
    for i in range(1, n_exp):
        spread(0, i)
        z_copy(1, sdy, at(dyall, 0, i), i, peer(i))
    spread(1, 0)
    spread(1, 1)
    loads[2].wait()
    loads[3].wait()
    forward(0)
    expert_out()
    for i in far_first:
        z_copy(2, ybuf, back.at[slots(i)], i, peer(i))
    for i in range(n_exp):
        relay(0, i)
    spread(1, 2)
    spread(1, 3)
    relay(1, 0)
    forward(1)
    spread(1, 4)
    relay(1, 1)
    forward(2)
    spread(1, 5)
    relay(1, 2)
    relay(1, 3)
    forward(3)
    spread(1, 6)
    spread(1, 7)
    relay(1, 4)
    relay(1, 5)
    backward(0)
    relay(1, 6)
    relay(1, 7)
    backward(1)
    backward(2)
    for i in far_first:
        z_copies[2, i].wait_recv()
    out[...] = (
        gates
        * lax.dot_general(
            place[...], back[...], (((0,), (0,)), ((), ())), preferred_element_type=jnp.float32
        )
    ).astype(jnp.bfloat16)
    out_copy = pltpu.make_async_copy(out, out_hbm, in_sem.at[4])
    out_copy.start()
    backward(3)
    for c in z_copies.values():
        c.wait_send()
    for c in g_copies.values():
        c.wait_send()
    out_copy.wait()
    for h in range(hidden // TILE):
        for c in stores(h):
            c.wait()


def fused(latent, cotangent, routes, gates, w_in, w_out, n_exp, cap):
    tok, width = latent.shape
    hidden = w_out.shape[2]
    rows = n_exp * cap
    share = width // 4
    bf16, f32 = jnp.bfloat16, jnp.float32
    vmem = pl.BlockSpec(memory_space=pltpu.VMEM)
    hbm = pl.BlockSpec(memory_space=pltpu.HBM)
    flops = 2 * rows * width * hidden * 16
    shapes = (
        jax.ShapeDtypeStruct((tok, width), bf16),
        jax.ShapeDtypeStruct((share, 2 * hidden), f32),
        jax.ShapeDtypeStruct((share, hidden), f32),
    )
    output, grad_in, grad_out = pl.pallas_call(
        functools.partial(fused_kernel, n_exp, cap),
        out_shape=shapes,
        in_specs=[hbm, hbm, vmem, vmem, hbm, hbm],
        out_specs=(hbm, hbm, hbm),
        scratch_shapes=[
            pltpu.VMEM((tok, width), bf16),
            pltpu.VMEM((share, 2 * hidden), f32),
            pltpu.VMEM((share, hidden), f32),
            pltpu.VMEM((tok, width), bf16),
            pltpu.VMEM((tok, width), bf16),
            pltpu.VMEM((width, 2 * hidden), bf16),
            pltpu.VMEM((width, hidden), bf16),
            pltpu.VMEM((rows, width), bf16),
            pltpu.VMEM((rows, width), bf16),
            pltpu.VMEM((4, rows, width), bf16),
            pltpu.VMEM((4, rows, width), bf16),
            pltpu.VMEM((4, rows, hidden), f32),
            pltpu.VMEM((4, rows, hidden), f32),
            pltpu.VMEM((4, rows, hidden), bf16),
            pltpu.VMEM((rows, width), bf16),
            pltpu.VMEM((rows, width), bf16),
            pltpu.VMEM((rows, tok), bf16),
            pltpu.SemaphoreType.DMA((5,)),
            pltpu.SemaphoreType.DMA((3, hidden // TILE)),
            pltpu.SemaphoreType.DMA((3, n_exp)),
            pltpu.SemaphoreType.DMA((3, n_exp)),
            pltpu.SemaphoreType.DMA((2, 3, n_exp)),
            pltpu.SemaphoreType.DMA((2, 3, n_exp)),
        ],
        compiler_params=pltpu.CompilerParams(
            collective_id=0, has_side_effects=True, vmem_limit_bytes=60 * 1024 * 1024
        ),
        cost_estimate=pl.CostEstimate(
            flops=flops, bytes_accessed=10 * 1024 * 1024, transcendentals=4 * rows * hidden
        ),
    )(latent, cotangent, routes.reshape(1, tok), gates.reshape(1, tok), w_in, w_out)
    return output, grad_in.reshape(1, share, 2 * hidden), grad_out.reshape(1, share, hidden)


def on_device(latent, cotangent, routes, gates, w_in, w_out):
    n_experts = lax.axis_size("expert")
    n_replicas = lax.axis_size("dp")
    tok_count = latent.shape[0]
    top_count = routes.shape[1]
    width = latent.shape[1]
    hidden_units = w_out.shape[2]
    capacity = max(2, 2 * tok_count * top_count // n_experts)
    if n_replicas == 4 and top_count == 1 and capacity % 16 == 0 and tok_count == 128 and n_experts == 8:
        return fused(latent, cotangent, routes, gates, w_in, w_out, n_experts, capacity)
    route_flat = routes.reshape(-1)
    gate_flat = gates.reshape(-1)
    onehot = (route_flat[:, None] == jnp.arange(n_experts, dtype=jnp.int32)[None, :]).astype(
        jnp.int32
    )
    before = jnp.cumsum(onehot, axis=0) - onehot
    slot = jnp.sum(before * onehot, axis=1)
    position = route_flat * capacity + slot
    placing = (
        jnp.arange(n_experts * capacity, dtype=jnp.int32)[:, None] == position[None, :]
    ).astype(jnp.bfloat16)
    x_rows = jnp.repeat(latent, top_count, axis=0)
    dy_rows = (
        gate_flat[:, None] * jnp.repeat(cotangent, top_count, axis=0).astype(jnp.float32)
    ).astype(jnp.bfloat16)
    send_x = (
        jnp.dot(placing, x_rows, preferred_element_type=jnp.float32)
        .astype(jnp.bfloat16)
        .reshape(n_experts, capacity, width)
    )
    send_dy = (
        jnp.dot(placing, dy_rows, preferred_element_type=jnp.float32)
        .astype(jnp.bfloat16)
        .reshape(n_experts, capacity, width)
    )
    got_x = lax.all_to_all(send_x, "expert", split_axis=0, concat_axis=0, tiled=True)
    got_dy = None
    x_buf = got_x.reshape(-1, width)
    acts = jnp.dot(x_buf, w_in[0], preferred_element_type=jnp.float32)
    gate = acts[:, :hidden_units]
    upper = acts[:, hidden_units:]
    sig = jax.nn.sigmoid(gate)
    swish = gate * sig
    hidden = (swish * upper).astype(jnp.bfloat16)
    y_buf = lax.dot_general(
        hidden, w_out[0], (((1,), (1,)), ((), ())), preferred_element_type=jnp.float32
    ).astype(jnp.bfloat16)
    back = lax.all_to_all(
        y_buf.reshape(n_experts, capacity, width), "expert", split_axis=0, concat_axis=0, tiled=True
    ).reshape(-1, width)
    y_rows = lax.dot_general(
        placing, back, (((0,), (0,)), ((), ())), preferred_element_type=jnp.float32
    )
    output = jnp.sum(
        (gate_flat[:, None] * y_rows).reshape(tok_count, top_count, width), axis=1
    ).astype(jnp.bfloat16)
    got_dy = lax.all_to_all(send_dy, "expert", split_axis=0, concat_axis=0, tiled=True)
    dy_buf = got_dy.reshape(-1, width)
    d_hidden = jnp.dot(dy_buf, w_out[0], preferred_element_type=jnp.float32)
    d_gate = d_hidden * upper * sig * (1.0 + gate * (1.0 - sig))
    d_upper = d_hidden * swish
    d_acts = jnp.concatenate([d_gate, d_upper], axis=1).astype(jnp.bfloat16)
    share = width // n_replicas
    columns = x_buf
    grad_in = lax.psum_scatter(
        lax.dot_general(
            columns, d_acts, (((0,), (0,)), ((), ())), preferred_element_type=jnp.float32
        ).astype(jnp.bfloat16),
        "dp",
        scatter_dimension=0,
        tiled=True,
    ).astype(jnp.float32)
    columns = dy_buf
    grad_out = lax.psum_scatter(
        lax.dot_general(
            columns, hidden, (((0,), (0,)), ((), ())), preferred_element_type=jnp.float32
        ).astype(jnp.bfloat16),
        "dp",
        scatter_dimension=0,
        tiled=True,
    ).astype(jnp.float32)
    return (
        output,
        grad_in.reshape(1, share, 2 * hidden_units),
        grad_out.reshape(1, share, hidden_units),
    )


def solution(mesh):
    in_specs = (
        P(("dp", "expert"), None),
        P(("dp", "expert"), None),
        P(("dp", "expert"), None),
        P(("dp", "expert"), None),
        P("expert", None, None),
        P("expert", None, None),
    )
    out_specs = (P(("dp", "expert"), None), P("expert", "dp", None), P("expert", "dp", None))
    return jax.shard_map(
        on_device, mesh=mesh, in_specs=in_specs, out_specs=out_specs, check_vma=False
    )
```

```python
import functools

import jax
import jax.numpy as jnp
from jax import lax
from jax.experimental import pallas as pl
from jax.experimental.pallas import tpu as pltpu
from jax.sharding import PartitionSpec as P

MESH = pl.DeviceIdType.MESH
TILE = 256


def fused_kernel(
    n_exp, cap,
    lat_hbm, cot_hbm, routes_ref, gates_ref, win_hbm, wout_hbm,
    out_hbm, gin_hbm, gout_hbm, gin_last_hbm, gout_last_hbm,
    out, gin, gout, gin_last, gout_last, xt, dyt, lat, cot, win, wout, sx, sdy, xall, dyall, a1, a2, hid, ybuf, back, place,
    in_sem, out_sem, last_sem, zsend, zrecv, gsend, grecv,
):
    p = lax.axis_index("dp")
    q = lax.axis_index("expert")
    px, py = lax.rem(p, 2), lax.div(p, 2)
    xn = (py * 2 + 1 - px, q)
    yn = ((1 - py) * 2 + px, q)
    tok, width = lat.shape
    rows = n_exp * cap
    hidden = hid.shape[2]
    share = gin.shape[0]
    half = n_exp // 2
    z, core = lax.div(q, 2), lax.rem(q, 2)

    def partner_of(i):
        line = (z, z + 1 - 2 * lax.rem(z, 2), lax.rem(z + 2, 4), 3 - z)[i // 2]
        return line * 2 + (core if i % 2 == 0 else 1 - core)

    partners = [partner_of(i) for i in range(n_exp)]
    far_first = [4, 5, 6, 7, 2, 3, 1]

    def peer(i):
        return (p, partners[i])

    barrier = pltpu.get_barrier_semaphore()
    for i in range(1, n_exp):
        pl.semaphore_signal(barrier, inc=1, device_id=peer(i), device_id_type=MESH)
    pl.semaphore_signal(barrier, inc=1, device_id=xn, device_id_type=MESH)
    pl.semaphore_signal(barrier, inc=1, device_id=yn, device_id_type=MESH)
    loads = [
        pltpu.make_async_copy(src, dst, in_sem.at[n])
        for n, (src, dst) in enumerate(
            ((lat_hbm, lat), (cot_hbm, cot), (win_hbm.at[0], win), (wout_hbm.at[0], wout))
        )
    ]
    for c in loads:
        c.start()

    routes = routes_ref[...]
    index = jnp.zeros_like(routes)
    for i in range(1, n_exp):
        index = jnp.where(routes == partners[i], i, index)
    i0 = lax.broadcasted_iota(jnp.int32, (tok, tok), 0)
    i1 = lax.broadcasted_iota(jnp.int32, (tok, tok), 1)
    onehot = jnp.where(i0 == index, 1.0, 0.0)
    earlier = jnp.where(i0 < i1, 1.0, 0.0)
    before = jnp.dot(
        onehot.astype(jnp.bfloat16), earlier.astype(jnp.bfloat16), preferred_element_type=jnp.float32
    )
    slot = jnp.sum(before * onehot, axis=0, keepdims=True)
    position = index.astype(jnp.float32) * cap + slot
    place[...] = jnp.where(
        lax.broadcasted_iota(jnp.int32, (rows, tok), 0).astype(jnp.float32) == position, 1.0, 0.0
    ).astype(jnp.bfloat16)
    gates = jnp.sum(jnp.where(i0 == i1, gates_ref[...], 0.0), axis=1, keepdims=True)

    def place_rows(value, sent, kept):
        placed = jnp.dot(place[...], value, preferred_element_type=jnp.float32).astype(jnp.bfloat16)
        sent[...] = placed
        kept[0, 0:cap, :] = placed[0:cap, :]

    def at(buf, group, i):
        first = (group % 2) * (rows // 2) + (i % half) * cap
        return buf.at[i // half * 2 + group // 2, pl.ds(first, cap)]

    def slots(i):
        return pl.ds(i * cap, cap)

    def z_copy(kind, src, dst, i, to):
        c = pltpu.make_async_remote_copy(
            src_ref=src.at[slots(i)],
            dst_ref=dst,
            send_sem=zsend.at[kind, i],
            recv_sem=zrecv.at[kind, i],
            device_id=to,
            device_id_type=MESH,
        )
        z_copies[kind, i] = c
        c.start()

    buffers = (xall, dyall)
    z_copies, g_copies = {}, {}
    received = set()

    loads[0].wait()
    place_rows(lat[...], sx, xall)
    pl.semaphore_wait(barrier, n_exp + 1)
    for i in (1, 4, 2, 5, 3, 6, 7):
        z_copy(0, sx, at(xall, 0, i), i, peer(i))

    def g_copy(kind, src, dst, i, to):
        c = pltpu.make_async_remote_copy(
            src_ref=at(buffers[kind], src, i),
            dst_ref=at(buffers[kind], dst, i),
            send_sem=gsend.at[kind, dst - 1, i],
            recv_sem=grecv.at[kind, dst - 1, i],
            device_id=to,
            device_id_type=MESH,
        )
        g_copies[kind, dst, i] = c
        c.start()

    def take(kind, group, i):
        if (kind, group, i) not in received:
            received.add((kind, group, i))
            if group:
                g_copies[kind, group, i].wait_recv()
            elif i:
                z_copies[kind, i].wait_recv()

    def spread(kind, i):
        take(kind, 0, i)
        g_copy(kind, 0, 1, i, xn)
        g_copy(kind, 0, 2, i, yn)

    def relay(kind, i):
        if i % 2 == 0:
            take(kind, 1, i)
            g_copy(kind, 1, 3, i, yn)
        else:
            take(kind, 2, i)
            g_copy(kind, 2, 3, i, xn)

    def take_chunk(kind, c):
        for i in range(c // 2 * half, (c // 2 + 1) * half):
            take(kind, c % 2 * 2, i)
            take(kind, c % 2 * 2 + 1, i)

    def forward(c):
        take_chunk(0, c)

        @pl.loop(0, hidden // TILE)
        def _(h):
            lo = pl.ds(pl.multiple_of(h * TILE, TILE), TILE)
            hi = pl.ds(pl.multiple_of(hidden + h * TILE, TILE), TILE)
            gate = jnp.dot(xall[c], win[:, lo], preferred_element_type=jnp.float32)
            upper = jnp.dot(xall[c], win[:, hi], preferred_element_type=jnp.float32)
            sig = jax.nn.sigmoid(gate)
            swish = gate * sig
            hid[c, :, lo] = (swish * upper).astype(jnp.bfloat16)
            a1[c, :, lo] = upper * sig * (1.0 + gate * (1.0 - sig))
            a2[c, :, lo] = swish

    def backward(c):
        take_chunk(1, c)
        cols = pl.ds(pl.multiple_of(p * share, share), share)
        xt[...] = xall[c, :, cols].T
        dyt[...] = dyall[c, :, cols].T

        @pl.loop(0, hidden // TILE)
        def _(h):
            lo = pl.ds(pl.multiple_of(h * TILE, TILE), TILE)
            hi = pl.ds(pl.multiple_of(hidden + h * TILE, TILE), TILE)
            d_hid = jnp.dot(dyall[c], wout[:, lo], preferred_element_type=jnp.float32)
            d_gate = (d_hid * a1[c, :, lo]).astype(jnp.bfloat16)
            d_upper = (d_hid * a2[c, :, lo]).astype(jnp.bfloat16)

            def add(total, last, where, left, right):
                term = jnp.dot(left[...], right, preferred_element_type=jnp.float32)
                if c == 3:
                    last[:, where] = term.astype(jnp.bfloat16)
                elif c == 0:
                    total[:, where] = term
                else:
                    total[:, where] += term

            add(gin, gin_last, lo, xt, d_gate)
            add(gin, gin_last, hi, xt, d_upper)
            add(gout, gout_last, lo, dyt, hid[c, :, lo])
            if c == 3:
                for copy in last_stores(h):
                    copy.start()

    def last_stores(h):
        lo = pl.ds(pl.multiple_of(h * TILE, TILE), TILE)
        hi = pl.ds(pl.multiple_of(hidden + h * TILE, TILE), TILE)
        parts = (
            (gin_last, gin_last_hbm, lo), (gin_last, gin_last_hbm, hi), (gout_last, gout_last_hbm, lo)
        )
        return [
            pltpu.make_async_copy(src.at[:, where], dst.at[:, where], last_sem.at[n, h])
            for n, (src, dst, where) in enumerate(parts)
        ]

    def expert_out():
        @pl.loop(0, width // TILE)
        def _(l):
            tile = pl.ds(pl.multiple_of(l * TILE, TILE), TILE)
            own = jnp.concatenate([hid[0, 0 : rows // 2, :], hid[2, 0 : rows // 2, :]], axis=0)
            ybuf[:, tile] = lax.dot_general(
                own, wout[tile, :], (((1,), (1,)), ((), ())), preferred_element_type=jnp.float32
            ).astype(jnp.bfloat16)

        back[0:cap, :] = ybuf[0:cap, :]

    spread(0, 0)
    loads[1].wait()
    place_rows((gates * cot[...].astype(jnp.float32)).astype(jnp.bfloat16), sdy, dyall)
    def send_dy(*which):
        for i in which:
            z_copy(1, sdy, at(dyall, 0, i), i, peer(i))

    send_dy(1, 2, 3)
    for i in range(1, half):
        spread(0, i)
    for i in range(half):
        spread(1, i)
    spread(0, 4)
    send_dy(4, 5)
    for i in range(half):
        relay(0, i)
    loads[2].wait()
    loads[3].wait()
    forward(0)
    spread(0, 5)
    send_dy(6, 7)
    relay(1, 0)
    relay(1, 1)
    forward(1)
    spread(0, 6)
    relay(1, 2)
    relay(1, 3)
    backward(0)
    spread(0, 7)
    relay(0, 4)
    relay(0, 5)
    backward(1)
    relay(0, 6)
    relay(0, 7)
    forward(2)
    spread(1, 4)
    spread(1, 5)
    expert_out()
    spread(1, 6)
    relay(1, 4)
    forward(3)
    spread(1, 7)
    relay(1, 5)
    for i in far_first:
        z_copy(2, ybuf, back.at[slots(i)], i, peer(i))
    relay(1, 6)
    relay(1, 7)
    backward(2)
    stores = [
        pltpu.make_async_copy(src, dst, out_sem.at[n])
        for n, (src, dst) in enumerate(((gin, gin_hbm), (gout, gout_hbm), (out, out_hbm)))
    ]
    stores[0].start()
    stores[1].start()
    backward(3)
    for i in far_first:
        z_copies[2, i].wait_recv()
    out[...] = lax.dot_general(
        place[...], back[...], (((0,), (0,)), ((), ())), preferred_element_type=jnp.float32
    ).astype(jnp.bfloat16)
    stores[2].start()
    for c in z_copies.values():
        c.wait_send()
    for c in g_copies.values():
        c.wait_send()
    for c in stores:
        c.wait()
    for h in range(hidden // TILE):
        for c in last_stores(h):
            c.wait()


def fused(latent, cotangent, routes, gates, w_in, w_out, n_exp, cap):
    tok, width = latent.shape
    hidden = w_out.shape[2]
    rows = n_exp * cap
    share = width // 4
    bf16, f32 = jnp.bfloat16, jnp.float32
    vmem = pl.BlockSpec(memory_space=pltpu.VMEM)
    hbm = pl.BlockSpec(memory_space=pltpu.HBM)
    flops = 2 * rows * width * hidden * 16
    shapes = (
        jax.ShapeDtypeStruct((tok, width), bf16),
        jax.ShapeDtypeStruct((share, 2 * hidden), f32),
        jax.ShapeDtypeStruct((share, hidden), f32),
        jax.ShapeDtypeStruct((share, 2 * hidden), bf16),
        jax.ShapeDtypeStruct((share, hidden), bf16),
    )
    y_rows, grad_in, grad_out, last_in, last_out = pl.pallas_call(
        functools.partial(fused_kernel, n_exp, cap),
        out_shape=shapes,
        in_specs=[hbm, hbm, vmem, vmem, hbm, hbm],
        out_specs=(hbm,) * 5,
        scratch_shapes=[
            pltpu.VMEM((tok, width), bf16),
            pltpu.VMEM((share, 2 * hidden), f32),
            pltpu.VMEM((share, hidden), f32),
            pltpu.VMEM((share, 2 * hidden), bf16),
            pltpu.VMEM((share, hidden), bf16),
            pltpu.VMEM((share, rows), bf16),
            pltpu.VMEM((share, rows), bf16),
            pltpu.VMEM((tok, width), bf16),
            pltpu.VMEM((tok, width), bf16),
            pltpu.VMEM((width, 2 * hidden), bf16),
            pltpu.VMEM((width, hidden), bf16),
            pltpu.VMEM((rows, width), bf16),
            pltpu.VMEM((rows, width), bf16),
            pltpu.VMEM((4, rows, width), bf16),
            pltpu.VMEM((4, rows, width), bf16),
            pltpu.VMEM((4, rows, hidden), f32),
            pltpu.VMEM((4, rows, hidden), f32),
            pltpu.VMEM((4, rows, hidden), bf16),
            pltpu.VMEM((rows, width), bf16),
            pltpu.VMEM((rows, width), bf16),
            pltpu.VMEM((rows, tok), bf16),
            pltpu.SemaphoreType.DMA((4,)),
            pltpu.SemaphoreType.DMA((3,)),
            pltpu.SemaphoreType.DMA((3, hidden // TILE)),
            pltpu.SemaphoreType.DMA((3, n_exp)),
            pltpu.SemaphoreType.DMA((3, n_exp)),
            pltpu.SemaphoreType.DMA((2, 3, n_exp)),
            pltpu.SemaphoreType.DMA((2, 3, n_exp)),
        ],
        compiler_params=pltpu.CompilerParams(
            collective_id=0, has_side_effects=True, vmem_limit_bytes=60 * 1024 * 1024
        ),
        cost_estimate=pl.CostEstimate(
            flops=flops, bytes_accessed=10 * 1024 * 1024, transcendentals=4 * rows * hidden
        ),
    )(latent, cotangent, routes.reshape(1, tok), gates.reshape(1, tok), w_in, w_out)
    output = (gates * y_rows.astype(f32)).astype(bf16)
    grad_in = grad_in + last_in.astype(f32)
    grad_out = grad_out + last_out.astype(f32)
    return output, grad_in.reshape(1, share, 2 * hidden), grad_out.reshape(1, share, hidden)


def on_device(latent, cotangent, routes, gates, w_in, w_out):
    n_experts = lax.axis_size("expert")
    n_replicas = lax.axis_size("dp")
    tok_count = latent.shape[0]
    top_count = routes.shape[1]
    width = latent.shape[1]
    hidden_units = w_out.shape[2]
    capacity = max(2, 2 * tok_count * top_count // n_experts)
    if n_replicas == 4 and top_count == 1 and capacity % 16 == 0 and tok_count == 128 and n_experts == 8:
        return fused(latent, cotangent, routes, gates, w_in, w_out, n_experts, capacity)
    route_flat = routes.reshape(-1)
    gate_flat = gates.reshape(-1)
    onehot = (route_flat[:, None] == jnp.arange(n_experts, dtype=jnp.int32)[None, :]).astype(
        jnp.int32
    )
    before = jnp.cumsum(onehot, axis=0) - onehot
    slot = jnp.sum(before * onehot, axis=1)
    position = route_flat * capacity + slot
    placing = (
        jnp.arange(n_experts * capacity, dtype=jnp.int32)[:, None] == position[None, :]
    ).astype(jnp.bfloat16)
    x_rows = jnp.repeat(latent, top_count, axis=0)
    dy_rows = (
        gate_flat[:, None] * jnp.repeat(cotangent, top_count, axis=0).astype(jnp.float32)
    ).astype(jnp.bfloat16)
    send_x = (
        jnp.dot(placing, x_rows, preferred_element_type=jnp.float32)
        .astype(jnp.bfloat16)
        .reshape(n_experts, capacity, width)
    )
    send_dy = (
        jnp.dot(placing, dy_rows, preferred_element_type=jnp.float32)
        .astype(jnp.bfloat16)
        .reshape(n_experts, capacity, width)
    )
    got_x = lax.all_to_all(send_x, "expert", split_axis=0, concat_axis=0, tiled=True)
    got_dy = None
    x_buf = got_x.reshape(-1, width)
    acts = jnp.dot(x_buf, w_in[0], preferred_element_type=jnp.float32)
    gate = acts[:, :hidden_units]
    upper = acts[:, hidden_units:]
    sig = jax.nn.sigmoid(gate)
    swish = gate * sig
    hidden = (swish * upper).astype(jnp.bfloat16)
    y_buf = lax.dot_general(
        hidden, w_out[0], (((1,), (1,)), ((), ())), preferred_element_type=jnp.float32
    ).astype(jnp.bfloat16)
    back = lax.all_to_all(
        y_buf.reshape(n_experts, capacity, width), "expert", split_axis=0, concat_axis=0, tiled=True
    ).reshape(-1, width)
    y_rows = lax.dot_general(
        placing, back, (((0,), (0,)), ((), ())), preferred_element_type=jnp.float32
    )
    output = jnp.sum(
        (gate_flat[:, None] * y_rows).reshape(tok_count, top_count, width), axis=1
    ).astype(jnp.bfloat16)
    got_dy = lax.all_to_all(send_dy, "expert", split_axis=0, concat_axis=0, tiled=True)
    dy_buf = got_dy.reshape(-1, width)
    d_hidden = jnp.dot(dy_buf, w_out[0], preferred_element_type=jnp.float32)
    d_gate = d_hidden * upper * sig * (1.0 + gate * (1.0 - sig))
    d_upper = d_hidden * swish
    d_acts = jnp.concatenate([d_gate, d_upper], axis=1).astype(jnp.bfloat16)
    share = width // n_replicas
    columns = x_buf
    grad_in = lax.psum_scatter(
        lax.dot_general(
            columns, d_acts, (((0,), (0,)), ((), ())), preferred_element_type=jnp.float32
        ).astype(jnp.bfloat16),
        "dp",
        scatter_dimension=0,
        tiled=True,
    ).astype(jnp.float32)
    columns = dy_buf
    grad_out = lax.psum_scatter(
        lax.dot_general(
            columns, hidden, (((0,), (0,)), ((), ())), preferred_element_type=jnp.float32
        ).astype(jnp.bfloat16),
        "dp",
        scatter_dimension=0,
        tiled=True,
    ).astype(jnp.float32)
    return (
        output,
        grad_in.reshape(1, share, 2 * hidden_units),
        grad_out.reshape(1, share, hidden_units),
    )


def solution(mesh):
    in_specs = (
        P(("dp", "expert"), None),
        P(("dp", "expert"), None),
        P(("dp", "expert"), None),
        P(("dp", "expert"), None),
        P("expert", None, None),
        P("expert", None, None),
    )
    out_specs = (P(("dp", "expert"), None), P("expert", "dp", None), P("expert", "dp", None))
    return jax.shard_map(
        on_device, mesh=mesh, in_specs=in_specs, out_specs=out_specs, check_vma=False
    )
```

```python
import functools

import jax
import jax.numpy as jnp
from jax import lax
from jax.experimental import pallas as pl
from jax.experimental.pallas import tpu as pltpu
from jax.sharding import PartitionSpec as P

MESH = pl.DeviceIdType.MESH
TILE = 256


def fused_kernel(
    n_exp, cap,
    lat_hbm, cot_hbm, routes_ref, gates_ref, win_hbm, wout_hbm,
    out_hbm, gin_hbm, gout_hbm,
    out, gin, gout, xt, dyt, lat, cot, win, wout, sx, sdy, xall, dyall, a1, a2, hid, ybuf, back, place,
    in_sem, out_sem, zsend, zrecv, gsend, grecv,
):
    p = lax.axis_index("dp")
    q = lax.axis_index("expert")
    px, py = lax.rem(p, 2), lax.div(p, 2)
    xn = (py * 2 + 1 - px, q)
    yn = ((1 - py) * 2 + px, q)
    tok, width = lat.shape
    rows = n_exp * cap
    hidden = hid.shape[2]
    share = gin.shape[0]
    half = n_exp // 2
    z, core = lax.div(q, 2), lax.rem(q, 2)

    def partner_of(i):
        line = (z, z + 1 - 2 * lax.rem(z, 2), lax.rem(z + 2, 4), 3 - z)[i // 2]
        return line * 2 + (core if i % 2 == 0 else 1 - core)

    partners = [partner_of(i) for i in range(n_exp)]
    far_first = [4, 5, 6, 7, 2, 3, 1]

    def peer(i):
        return (p, partners[i])

    barrier = pltpu.get_barrier_semaphore()
    for i in range(1, n_exp):
        pl.semaphore_signal(barrier, inc=1, device_id=peer(i), device_id_type=MESH)
    pl.semaphore_signal(barrier, inc=1, device_id=xn, device_id_type=MESH)
    pl.semaphore_signal(barrier, inc=1, device_id=yn, device_id_type=MESH)
    loads = [
        pltpu.make_async_copy(src, dst, in_sem.at[n])
        for n, (src, dst) in enumerate(
            ((lat_hbm, lat), (cot_hbm, cot), (win_hbm.at[0], win), (wout_hbm.at[0], wout))
        )
    ]
    for c in loads:
        c.start()

    routes = routes_ref[...]
    index = jnp.zeros_like(routes)
    for i in range(1, n_exp):
        index = jnp.where(routes == partners[i], i, index)
    i0 = lax.broadcasted_iota(jnp.int32, (tok, tok), 0)
    i1 = lax.broadcasted_iota(jnp.int32, (tok, tok), 1)
    onehot = jnp.where(i0 == index, 1.0, 0.0)
    earlier = jnp.where(i0 < i1, 1.0, 0.0)
    before = jnp.dot(
        onehot.astype(jnp.bfloat16), earlier.astype(jnp.bfloat16), preferred_element_type=jnp.float32
    )
    slot = jnp.sum(before * onehot, axis=0, keepdims=True)
    position = index.astype(jnp.float32) * cap + slot
    place[...] = jnp.where(
        lax.broadcasted_iota(jnp.int32, (rows, tok), 0).astype(jnp.float32) == position, 1.0, 0.0
    ).astype(jnp.bfloat16)
    gates = jnp.sum(jnp.where(i0 == i1, gates_ref[...], 0.0), axis=1, keepdims=True)

    def place_rows(value, sent, kept):
        placed = jnp.dot(place[...], value, preferred_element_type=jnp.float32).astype(jnp.bfloat16)
        sent[...] = placed
        kept[0, 0:cap, :] = placed[0:cap, :]

    def at(buf, group, i):
        if group in (0, 3):
            return buf.at[group, pl.ds(i * cap, cap)]
        return buf.at[1 + i // half, pl.ds((group - 1) * (rows // 2) + (i % half) * cap, cap)]

    def slots(i):
        return pl.ds(i * cap, cap)

    def z_copy(kind, src, dst, i, to):
        c = pltpu.make_async_remote_copy(
            src_ref=src.at[slots(i)],
            dst_ref=dst,
            send_sem=zsend.at[kind, i],
            recv_sem=zrecv.at[kind, i],
            device_id=to,
            device_id_type=MESH,
        )
        z_copies[kind, i] = c
        c.start()

    buffers = (xall, dyall)
    z_copies, g_copies = {}, {}
    received = set()

    loads[0].wait()
    place_rows(lat[...], sx, xall)
    pl.semaphore_wait(barrier, n_exp + 1)
    for i in (1, 4, 2, 5, 3, 6, 7):
        z_copy(0, sx, at(xall, 0, i), i, peer(i))

    def g_copy(kind, src, dst, i, to):
        c = pltpu.make_async_remote_copy(
            src_ref=at(buffers[kind], src, i),
            dst_ref=at(buffers[kind], dst, i),
            send_sem=gsend.at[kind, dst - 1, i],
            recv_sem=grecv.at[kind, dst - 1, i],
            device_id=to,
            device_id_type=MESH,
        )
        g_copies[kind, dst, i] = c
        c.start()

    def take(kind, group, i):
        if (kind, group, i) not in received:
            received.add((kind, group, i))
            if group:
                g_copies[kind, group, i].wait_recv()
            elif i:
                z_copies[kind, i].wait_recv()

    def spread(kind, i):
        take(kind, 0, i)
        g_copy(kind, 0, 1, i, xn)
        g_copy(kind, 0, 2, i, yn)

    def relay(kind, i):
        if i % 2 == 0:
            take(kind, 1, i)
            g_copy(kind, 1, 3, i, yn)
        else:
            take(kind, 2, i)
            g_copy(kind, 2, 3, i, xn)

    def take_chunk(kind, c):
        if c in (0, 3):
            for i in range(n_exp):
                take(kind, c, i)
        else:
            for i in range((c - 1) * half, c * half):
                take(kind, 1, i)
                take(kind, 2, i)

    def forward(c):
        take_chunk(0, c)

        @pl.loop(0, hidden // TILE)
        def _(h):
            lo = pl.ds(pl.multiple_of(h * TILE, TILE), TILE)
            hi = pl.ds(pl.multiple_of(hidden + h * TILE, TILE), TILE)
            gate = jnp.dot(xall[c], win[:, lo], preferred_element_type=jnp.float32)
            upper = jnp.dot(xall[c], win[:, hi], preferred_element_type=jnp.float32)
            sig = jax.nn.sigmoid(gate)
            swish = gate * sig
            hid[c, :, lo] = (swish * upper).astype(jnp.bfloat16)
            a1[c, :, lo] = upper * sig * (1.0 + gate * (1.0 - sig))
            a2[c, :, lo] = swish

    def backward(c):
        take_chunk(1, c)
        cols = pl.ds(pl.multiple_of(p * share, share), share)
        xt[...] = xall[c, :, cols].T
        dyt[...] = dyall[c, :, cols].T

        @pl.loop(0, hidden // TILE)
        def _(h):
            lo = pl.ds(pl.multiple_of(h * TILE, TILE), TILE)
            hi = pl.ds(pl.multiple_of(hidden + h * TILE, TILE), TILE)
            d_hid = jnp.dot(dyall[c], wout[:, lo], preferred_element_type=jnp.float32)
            d_gate = (d_hid * a1[c, :, lo]).astype(jnp.bfloat16)
            d_upper = (d_hid * a2[c, :, lo]).astype(jnp.bfloat16)

            def add(ref, where, left, right):
                term = jnp.dot(left[...], right, preferred_element_type=jnp.float32)
                ref[:, where] = term if c == 1 else ref[:, where] + term

            add(gin, lo, xt, d_gate)
            add(gin, hi, xt, d_upper)
            add(gout, lo, dyt, hid[c, :, lo])
            if c == 3:
                for copy in stores(h):
                    copy.start()

    def stores(h):
        lo = pl.ds(pl.multiple_of(h * TILE, TILE), TILE)
        hi = pl.ds(pl.multiple_of(hidden + h * TILE, TILE), TILE)
        pairs = ((gin, gin_hbm, lo), (gin, gin_hbm, hi), (gout, gout_hbm, lo))
        return [
            pltpu.make_async_copy(src.at[:, where], dst.at[:, where], out_sem.at[n, h])
            for n, (src, dst, where) in enumerate(pairs)
        ]

    def expert_out():
        @pl.loop(0, width // TILE)
        def _(l):
            tile = pl.ds(pl.multiple_of(l * TILE, TILE), TILE)
            ybuf[:, tile] = lax.dot_general(
                hid[0], wout[tile, :], (((1,), (1,)), ((), ())), preferred_element_type=jnp.float32
            ).astype(jnp.bfloat16)

        back[0:cap, :] = ybuf[0:cap, :]

    spread(0, 0)
    loads[1].wait()
    place_rows((gates * cot[...].astype(jnp.float32)).astype(jnp.bfloat16), sdy, dyall)
    def send_dy(*which):
        for i in which:
            z_copy(1, sdy, at(dyall, 0, i), i, peer(i))

    def relays(kind, *which):
        for i in which:
            relay(kind, i)

    send_dy(1, 2, 3)
    spread(0, 1)
    spread(0, 2)
    spread(0, 3)
    spread(1, 0)
    spread(1, 1)
    spread(0, 4)
    send_dy(4, 5)
    relays(0, 0, 1)
    spread(0, 5)
    send_dy(6, 7)
    spread(1, 2)
    spread(1, 3)
    relays(0, 2, 3)
    spread(0, 6)
    spread(0, 7)
    loads[2].wait()
    loads[3].wait()
    forward(0)
    expert_out()
    relays(0, 4, 5)
    for i in far_first:
        z_copy(2, ybuf, back.at[slots(i)], i, peer(i))
    relays(1, 0, 1)
    spread(1, 4)
    relays(0, 6, 7)
    forward(1)
    spread(1, 5)
    relays(1, 2, 3)
    forward(2)
    spread(1, 6)
    relay(1, 4)
    forward(3)
    spread(1, 7)
    relay(1, 5)
    backward(1)
    relays(1, 6, 7)
    backward(0)
    backward(2)
    backward(3)
    for i in far_first:
        z_copies[2, i].wait_recv()
    out[...] = (
        gates
        * lax.dot_general(
            place[...], back[...], (((0,), (0,)), ((), ())), preferred_element_type=jnp.float32
        )
    ).astype(jnp.bfloat16)
    out_copy = pltpu.make_async_copy(out, out_hbm, in_sem.at[4])
    out_copy.start()
    for c in z_copies.values():
        c.wait_send()
    for c in g_copies.values():
        c.wait_send()
    out_copy.wait()
    for h in range(hidden // TILE):
        for c in stores(h):
            c.wait()


def fused(latent, cotangent, routes, gates, w_in, w_out, n_exp, cap):
    tok, width = latent.shape
    hidden = w_out.shape[2]
    rows = n_exp * cap
    share = width // 4
    bf16, f32 = jnp.bfloat16, jnp.float32
    vmem = pl.BlockSpec(memory_space=pltpu.VMEM)
    hbm = pl.BlockSpec(memory_space=pltpu.HBM)
    flops = 2 * rows * width * hidden * 16
    shapes = (
        jax.ShapeDtypeStruct((tok, width), bf16),
        jax.ShapeDtypeStruct((share, 2 * hidden), f32),
        jax.ShapeDtypeStruct((share, hidden), f32),
    )
    output, grad_in, grad_out = pl.pallas_call(
        functools.partial(fused_kernel, n_exp, cap),
        out_shape=shapes,
        in_specs=[hbm, hbm, vmem, vmem, hbm, hbm],
        out_specs=(hbm, hbm, hbm),
        scratch_shapes=[
            pltpu.VMEM((tok, width), bf16),
            pltpu.VMEM((share, 2 * hidden), f32),
            pltpu.VMEM((share, hidden), f32),
            pltpu.VMEM((share, rows), bf16),
            pltpu.VMEM((share, rows), bf16),
            pltpu.VMEM((tok, width), bf16),
            pltpu.VMEM((tok, width), bf16),
            pltpu.VMEM((width, 2 * hidden), bf16),
            pltpu.VMEM((width, hidden), bf16),
            pltpu.VMEM((rows, width), bf16),
            pltpu.VMEM((rows, width), bf16),
            pltpu.VMEM((4, rows, width), bf16),
            pltpu.VMEM((4, rows, width), bf16),
            pltpu.VMEM((4, rows, hidden), f32),
            pltpu.VMEM((4, rows, hidden), f32),
            pltpu.VMEM((4, rows, hidden), bf16),
            pltpu.VMEM((rows, width), bf16),
            pltpu.VMEM((rows, width), bf16),
            pltpu.VMEM((rows, tok), bf16),
            pltpu.SemaphoreType.DMA((5,)),
            pltpu.SemaphoreType.DMA((3, hidden // TILE)),
            pltpu.SemaphoreType.DMA((3, n_exp)),
            pltpu.SemaphoreType.DMA((3, n_exp)),
            pltpu.SemaphoreType.DMA((2, 3, n_exp)),
            pltpu.SemaphoreType.DMA((2, 3, n_exp)),
        ],
        compiler_params=pltpu.CompilerParams(
            collective_id=0, has_side_effects=True, vmem_limit_bytes=56 * 1024 * 1024
        ),
        cost_estimate=pl.CostEstimate(
            flops=flops, bytes_accessed=10 * 1024 * 1024, transcendentals=4 * rows * hidden
        ),
    )(latent, cotangent, routes.reshape(1, tok), gates.reshape(1, tok), w_in, w_out)
    return output, grad_in.reshape(1, share, 2 * hidden), grad_out.reshape(1, share, hidden)


def on_device(latent, cotangent, routes, gates, w_in, w_out):
    n_experts = lax.axis_size("expert")
    n_replicas = lax.axis_size("dp")
    tok_count = latent.shape[0]
    top_count = routes.shape[1]
    width = latent.shape[1]
    hidden_units = w_out.shape[2]
    capacity = max(2, 2 * tok_count * top_count // n_experts)
    if n_replicas == 4 and top_count == 1 and capacity % 16 == 0 and tok_count == 128 and n_experts == 8:
        return fused(latent, cotangent, routes, gates, w_in, w_out, n_experts, capacity)
    route_flat = routes.reshape(-1)
    gate_flat = gates.reshape(-1)
    onehot = (route_flat[:, None] == jnp.arange(n_experts, dtype=jnp.int32)[None, :]).astype(
        jnp.int32
    )
    before = jnp.cumsum(onehot, axis=0) - onehot
    slot = jnp.sum(before * onehot, axis=1)
    position = route_flat * capacity + slot
    placing = (
        jnp.arange(n_experts * capacity, dtype=jnp.int32)[:, None] == position[None, :]
    ).astype(jnp.bfloat16)
    x_rows = jnp.repeat(latent, top_count, axis=0)
    dy_rows = (
        gate_flat[:, None] * jnp.repeat(cotangent, top_count, axis=0).astype(jnp.float32)
    ).astype(jnp.bfloat16)
    send_x = (
        jnp.dot(placing, x_rows, preferred_element_type=jnp.float32)
        .astype(jnp.bfloat16)
        .reshape(n_experts, capacity, width)
    )
    send_dy = (
        jnp.dot(placing, dy_rows, preferred_element_type=jnp.float32)
        .astype(jnp.bfloat16)
        .reshape(n_experts, capacity, width)
    )
    got_x = lax.all_to_all(send_x, "expert", split_axis=0, concat_axis=0, tiled=True)
    got_dy = None
    x_buf = got_x.reshape(-1, width)
    acts = jnp.dot(x_buf, w_in[0], preferred_element_type=jnp.float32)
    gate = acts[:, :hidden_units]
    upper = acts[:, hidden_units:]
    sig = jax.nn.sigmoid(gate)
    swish = gate * sig
    hidden = (swish * upper).astype(jnp.bfloat16)
    y_buf = lax.dot_general(
        hidden, w_out[0], (((1,), (1,)), ((), ())), preferred_element_type=jnp.float32
    ).astype(jnp.bfloat16)
    back = lax.all_to_all(
        y_buf.reshape(n_experts, capacity, width), "expert", split_axis=0, concat_axis=0, tiled=True
    ).reshape(-1, width)
    y_rows = lax.dot_general(
        placing, back, (((0,), (0,)), ((), ())), preferred_element_type=jnp.float32
    )
    output = jnp.sum(
        (gate_flat[:, None] * y_rows).reshape(tok_count, top_count, width), axis=1
    ).astype(jnp.bfloat16)
    got_dy = lax.all_to_all(send_dy, "expert", split_axis=0, concat_axis=0, tiled=True)
    dy_buf = got_dy.reshape(-1, width)
    d_hidden = jnp.dot(dy_buf, w_out[0], preferred_element_type=jnp.float32)
    d_gate = d_hidden * upper * sig * (1.0 + gate * (1.0 - sig))
    d_upper = d_hidden * swish
    d_acts = jnp.concatenate([d_gate, d_upper], axis=1).astype(jnp.bfloat16)
    share = width // n_replicas
    columns = x_buf
    grad_in = lax.psum_scatter(
        lax.dot_general(
            columns, d_acts, (((0,), (0,)), ((), ())), preferred_element_type=jnp.float32
        ).astype(jnp.bfloat16),
        "dp",
        scatter_dimension=0,
        tiled=True,
    ).astype(jnp.float32)
    columns = dy_buf
    grad_out = lax.psum_scatter(
        lax.dot_general(
            columns, hidden, (((0,), (0,)), ((), ())), preferred_element_type=jnp.float32
        ).astype(jnp.bfloat16),
        "dp",
        scatter_dimension=0,
        tiled=True,
    ).astype(jnp.float32)
    return (
        output,
        grad_in.reshape(1, share, 2 * hidden_units),
        grad_out.reshape(1, share, hidden_units),
    )


def solution(mesh):
    in_specs = (
        P(("dp", "expert"), None),
        P(("dp", "expert"), None),
        P(("dp", "expert"), None),
        P(("dp", "expert"), None),
        P("expert", None, None),
        P("expert", None, None),
    )
    out_specs = (P(("dp", "expert"), None), P("expert", "dp", None), P("expert", "dp", None))
    return jax.shard_map(
        on_device, mesh=mesh, in_specs=in_specs, out_specs=out_specs, check_vma=False
    )
```

```python
import functools

import jax
import jax.numpy as jnp
from jax import lax
from jax.experimental import pallas as pl
from jax.experimental.pallas import tpu as pltpu
from jax.sharding import PartitionSpec as P

MESH = pl.DeviceIdType.MESH
TILE = 256


def fused_kernel(
    n_exp, cap,
    lat_hbm, cot_hbm, routes_ref, gates_ref, win_hbm, wout_hbm,
    out_hbm, gin_hbm, gout_hbm,
    out, gin, gout, xt, dyt, lat, cot, win, wout, sx, sdy, xall, dyall, a1, a2, hid, ybuf, back, place,
    in_sem, out_sem, zsend, zrecv, gsend, grecv,
):
    p = lax.axis_index("dp")
    q = lax.axis_index("expert")
    px, py = lax.rem(p, 2), lax.div(p, 2)
    xn = (py * 2 + 1 - px, q)
    yn = ((1 - py) * 2 + px, q)
    tok, width = lat.shape
    rows = n_exp * cap
    hidden = hid.shape[1]
    share = gin.shape[0]
    half = n_exp // 2
    z, core = lax.div(q, 2), lax.rem(q, 2)

    def partner_of(i):
        line = (z, z + 1 - 2 * lax.rem(z, 2), lax.rem(z + 2, 4), 3 - z)[i // 2]
        return line * 2 + (core if i % 2 == 0 else 1 - core)

    partners = [partner_of(i) for i in range(n_exp)]
    far_first = [4, 5, 6, 7, 2, 3, 1]

    def peer(i):
        return (p, partners[i])

    barrier = pltpu.get_barrier_semaphore()
    for i in range(1, n_exp):
        pl.semaphore_signal(barrier, inc=1, device_id=peer(i), device_id_type=MESH)
    pl.semaphore_signal(barrier, inc=1, device_id=xn, device_id_type=MESH)
    pl.semaphore_signal(barrier, inc=1, device_id=yn, device_id_type=MESH)
    loads = [
        pltpu.make_async_copy(src, dst, in_sem.at[n])
        for n, (src, dst) in enumerate(
            ((lat_hbm, lat), (cot_hbm, cot), (win_hbm.at[0], win), (wout_hbm.at[0], wout))
        )
    ]
    for c in loads:
        c.start()

    routes = routes_ref[...]
    index = jnp.zeros_like(routes)
    for i in range(1, n_exp):
        index = jnp.where(routes == partners[i], i, index)
    i0 = lax.broadcasted_iota(jnp.int32, (tok, tok), 0)
    i1 = lax.broadcasted_iota(jnp.int32, (tok, tok), 1)
    onehot = jnp.where(i0 == index, 1.0, 0.0)
    earlier = jnp.where(i0 < i1, 1.0, 0.0)
    before = jnp.dot(
        onehot.astype(jnp.bfloat16), earlier.astype(jnp.bfloat16), preferred_element_type=jnp.float32
    )
    slot = jnp.sum(before * onehot, axis=0, keepdims=True)
    position = index.astype(jnp.float32) * cap + slot
    place[...] = jnp.where(
        lax.broadcasted_iota(jnp.int32, (rows, tok), 0).astype(jnp.float32) == position, 1.0, 0.0
    ).astype(jnp.bfloat16)
    gates = jnp.sum(jnp.where(i0 == i1, gates_ref[...], 0.0), axis=1, keepdims=True)

    def place_rows(value, sent, kept):
        placed = jnp.dot(place[...], value, preferred_element_type=jnp.float32).astype(jnp.bfloat16)
        sent[...] = placed
        kept[0:cap, :] = placed[0:cap, :]

    spans = (pl.ds(0, rows), pl.ds(rows, rows * 3 // 2), pl.ds(rows * 5 // 2, rows * 3 // 2))

    def at(buf, group, i):
        if group == 0:
            return buf.at[pl.ds(i * cap, cap)]
        first = rows + (i // half) * (rows * 3 // 2) + (group - 1) * (rows // 2) + (i % half) * cap
        return buf.at[pl.ds(first, cap)]

    def slots(i):
        return pl.ds(i * cap, cap)

    def z_copy(kind, src, dst, i, to):
        c = pltpu.make_async_remote_copy(
            src_ref=src.at[slots(i)],
            dst_ref=dst,
            send_sem=zsend.at[kind, i],
            recv_sem=zrecv.at[kind, i],
            device_id=to,
            device_id_type=MESH,
        )
        z_copies[kind, i] = c
        c.start()

    buffers = (xall, dyall)
    z_copies, g_copies = {}, {}
    received = set()

    loads[0].wait()
    place_rows(lat[...], sx, xall)
    pl.semaphore_wait(barrier, n_exp + 1)
    for i in (1, 4, 2, 5, 3, 6, 7):
        z_copy(0, sx, at(xall, 0, i), i, peer(i))

    def g_copy(kind, src, dst, i, to):
        c = pltpu.make_async_remote_copy(
            src_ref=at(buffers[kind], src, i),
            dst_ref=at(buffers[kind], dst, i),
            send_sem=gsend.at[kind, dst - 1, i],
            recv_sem=grecv.at[kind, dst - 1, i],
            device_id=to,
            device_id_type=MESH,
        )
        g_copies[kind, dst, i] = c
        c.start()

    def take(kind, group, i):
        if (kind, group, i) not in received:
            received.add((kind, group, i))
            if group:
                g_copies[kind, group, i].wait_recv()
            elif i:
                z_copies[kind, i].wait_recv()

    def spread(kind, i):
        take(kind, 0, i)
        g_copy(kind, 0, 1, i, xn)
        g_copy(kind, 0, 2, i, yn)

    def relay(kind, i):
        if i % 2 == 0:
            take(kind, 1, i)
            g_copy(kind, 1, 3, i, yn)
        else:
            take(kind, 2, i)
            g_copy(kind, 2, 3, i, xn)

    def take_chunk(kind, c):
        for i in range(n_exp) if c == 0 else range((c - 1) * half, c * half):
            for group in (0,) if c == 0 else (1, 2, 3):
                take(kind, group, i)

    def forward(c):
        take_chunk(0, c)
        span = spans[c]

        @pl.loop(0, hidden // TILE)
        def _(h):
            lo = pl.ds(pl.multiple_of(h * TILE, TILE), TILE)
            hi = pl.ds(pl.multiple_of(hidden + h * TILE, TILE), TILE)
            gate = jnp.dot(xall[span, :], win[:, lo], preferred_element_type=jnp.float32)
            upper = jnp.dot(xall[span, :], win[:, hi], preferred_element_type=jnp.float32)
            sig = jax.nn.sigmoid(gate)
            swish = gate * sig
            hid[span, lo] = (swish * upper).astype(jnp.bfloat16)
            a1[span, lo] = upper * sig * (1.0 + gate * (1.0 - sig))
            a2[span, lo] = swish

    def backward(c):
        take_chunk(1, c)
        span = spans[c]
        count = span.size
        cols = pl.ds(pl.multiple_of(p * share, share), share)
        xt[:, 0:count] = xall[span, cols].T
        dyt[:, 0:count] = dyall[span, cols].T

        @pl.loop(0, hidden // TILE)
        def _(h):
            lo = pl.ds(pl.multiple_of(h * TILE, TILE), TILE)
            hi = pl.ds(pl.multiple_of(hidden + h * TILE, TILE), TILE)
            d_hid = jnp.dot(dyall[span, :], wout[:, lo], preferred_element_type=jnp.float32)
            d_gate = (d_hid * a1[span, lo]).astype(jnp.bfloat16)
            d_upper = (d_hid * a2[span, lo]).astype(jnp.bfloat16)

            def add(ref, where, left, right):
                term = jnp.dot(left[:, 0:count], right, preferred_element_type=jnp.float32)
                ref[:, where] = term if c == 0 else ref[:, where] + term

            add(gin, lo, xt, d_gate)
            add(gin, hi, xt, d_upper)
            add(gout, lo, dyt, hid[span, lo])
            if c == 2:
                for copy in stores(h):
                    copy.start()

    def stores(h):
        lo = pl.ds(pl.multiple_of(h * TILE, TILE), TILE)
        hi = pl.ds(pl.multiple_of(hidden + h * TILE, TILE), TILE)
        pairs = ((gin, gin_hbm, lo), (gin, gin_hbm, hi), (gout, gout_hbm, lo))
        return [
            pltpu.make_async_copy(src.at[:, where], dst.at[:, where], out_sem.at[n, h])
            for n, (src, dst, where) in enumerate(pairs)
        ]

    def expert_out():
        @pl.loop(0, width // TILE)
        def _(l):
            tile = pl.ds(pl.multiple_of(l * TILE, TILE), TILE)
            ybuf[:, tile] = lax.dot_general(
                hid[spans[0], :], wout[tile, :], (((1,), (1,)), ((), ())), preferred_element_type=jnp.float32
            ).astype(jnp.bfloat16)

        back[0:cap, :] = ybuf[0:cap, :]

    spread(0, 0)
    loads[1].wait()
    place_rows((gates * cot[...].astype(jnp.float32)).astype(jnp.bfloat16), sdy, dyall)
    def send_dy(*which):
        for i in which:
            z_copy(1, sdy, at(dyall, 0, i), i, peer(i))

    def relays(kind, *which):
        for i in which:
            relay(kind, i)

    send_dy(1, 2, 3)
    spread(0, 1)
    spread(0, 2)
    spread(0, 3)
    spread(1, 0)
    spread(1, 1)
    spread(0, 4)
    send_dy(4, 5)
    relays(0, 0, 1)
    spread(0, 5)
    send_dy(6, 7)
    spread(1, 2)
    spread(1, 3)
    relays(0, 2, 3)
    spread(0, 6)
    spread(0, 7)
    loads[2].wait()
    loads[3].wait()
    forward(0)
    expert_out()
    relays(0, 4, 5)
    for i in far_first:
        z_copy(2, ybuf, back.at[slots(i)], i, peer(i))
    relays(1, 0, 1)
    spread(1, 4)
    relays(0, 6, 7)
    forward(1)
    spread(1, 5)
    relays(1, 2, 3)
    forward(2)
    spread(1, 6)
    relay(1, 4)
    spread(1, 7)
    relay(1, 5)
    backward(0)
    relays(1, 6, 7)
    backward(1)
    backward(2)
    for i in far_first:
        z_copies[2, i].wait_recv()
    out[...] = (
        gates
        * lax.dot_general(
            place[...], back[...], (((0,), (0,)), ((), ())), preferred_element_type=jnp.float32
        )
    ).astype(jnp.bfloat16)
    out_copy = pltpu.make_async_copy(out, out_hbm, in_sem.at[4])
    out_copy.start()
    for c in z_copies.values():
        c.wait_send()
    for c in g_copies.values():
        c.wait_send()
    out_copy.wait()
    for h in range(hidden // TILE):
        for c in stores(h):
            c.wait()


def fused(latent, cotangent, routes, gates, w_in, w_out, n_exp, cap):
    tok, width = latent.shape
    hidden = w_out.shape[2]
    rows = n_exp * cap
    share = width // 4
    bf16, f32 = jnp.bfloat16, jnp.float32
    vmem = pl.BlockSpec(memory_space=pltpu.VMEM)
    hbm = pl.BlockSpec(memory_space=pltpu.HBM)
    flops = 2 * rows * width * hidden * 16
    shapes = (
        jax.ShapeDtypeStruct((tok, width), bf16),
        jax.ShapeDtypeStruct((share, 2 * hidden), f32),
        jax.ShapeDtypeStruct((share, hidden), f32),
    )
    output, grad_in, grad_out = pl.pallas_call(
        functools.partial(fused_kernel, n_exp, cap),
        out_shape=shapes,
        in_specs=[hbm, hbm, vmem, vmem, hbm, hbm],
        out_specs=(hbm, hbm, hbm),
        scratch_shapes=[
            pltpu.VMEM((tok, width), bf16),
            pltpu.VMEM((share, 2 * hidden), f32),
            pltpu.VMEM((share, hidden), f32),
            pltpu.VMEM((share, rows * 3 // 2), bf16),
            pltpu.VMEM((share, rows * 3 // 2), bf16),
            pltpu.VMEM((tok, width), bf16),
            pltpu.VMEM((tok, width), bf16),
            pltpu.VMEM((width, 2 * hidden), bf16),
            pltpu.VMEM((width, hidden), bf16),
            pltpu.VMEM((rows, width), bf16),
            pltpu.VMEM((rows, width), bf16),
            pltpu.VMEM((4 * rows, width), bf16),
            pltpu.VMEM((4 * rows, width), bf16),
            pltpu.VMEM((4 * rows, hidden), f32),
            pltpu.VMEM((4 * rows, hidden), f32),
            pltpu.VMEM((4 * rows, hidden), bf16),
            pltpu.VMEM((rows, width), bf16),
            pltpu.VMEM((rows, width), bf16),
            pltpu.VMEM((rows, tok), bf16),
            pltpu.SemaphoreType.DMA((5,)),
            pltpu.SemaphoreType.DMA((3, hidden // TILE)),
            pltpu.SemaphoreType.DMA((3, n_exp)),
            pltpu.SemaphoreType.DMA((3, n_exp)),
            pltpu.SemaphoreType.DMA((2, 3, n_exp)),
            pltpu.SemaphoreType.DMA((2, 3, n_exp)),
        ],
        compiler_params=pltpu.CompilerParams(
            collective_id=0, has_side_effects=True, vmem_limit_bytes=60 * 1024 * 1024
        ),
        cost_estimate=pl.CostEstimate(
            flops=flops, bytes_accessed=10 * 1024 * 1024, transcendentals=4 * rows * hidden
        ),
    )(latent, cotangent, routes.reshape(1, tok), gates.reshape(1, tok), w_in, w_out)
    return output, grad_in.reshape(1, share, 2 * hidden), grad_out.reshape(1, share, hidden)


def on_device(latent, cotangent, routes, gates, w_in, w_out):
    n_experts = lax.axis_size("expert")
    n_replicas = lax.axis_size("dp")
    tok_count = latent.shape[0]
    top_count = routes.shape[1]
    width = latent.shape[1]
    hidden_units = w_out.shape[2]
    capacity = max(2, 2 * tok_count * top_count // n_experts)
    if n_replicas == 4 and top_count == 1 and capacity % 16 == 0 and tok_count == 128 and n_experts == 8:
        return fused(latent, cotangent, routes, gates, w_in, w_out, n_experts, capacity)
    route_flat = routes.reshape(-1)
    gate_flat = gates.reshape(-1)
    onehot = (route_flat[:, None] == jnp.arange(n_experts, dtype=jnp.int32)[None, :]).astype(
        jnp.int32
    )
    before = jnp.cumsum(onehot, axis=0) - onehot
    slot = jnp.sum(before * onehot, axis=1)
    position = route_flat * capacity + slot
    placing = (
        jnp.arange(n_experts * capacity, dtype=jnp.int32)[:, None] == position[None, :]
    ).astype(jnp.bfloat16)
    x_rows = jnp.repeat(latent, top_count, axis=0)
    dy_rows = (
        gate_flat[:, None] * jnp.repeat(cotangent, top_count, axis=0).astype(jnp.float32)
    ).astype(jnp.bfloat16)
    send_x = (
        jnp.dot(placing, x_rows, preferred_element_type=jnp.float32)
        .astype(jnp.bfloat16)
        .reshape(n_experts, capacity, width)
    )
    send_dy = (
        jnp.dot(placing, dy_rows, preferred_element_type=jnp.float32)
        .astype(jnp.bfloat16)
        .reshape(n_experts, capacity, width)
    )
    got_x = lax.all_to_all(send_x, "expert", split_axis=0, concat_axis=0, tiled=True)
    got_dy = None
    x_buf = got_x.reshape(-1, width)
    acts = jnp.dot(x_buf, w_in[0], preferred_element_type=jnp.float32)
    gate = acts[:, :hidden_units]
    upper = acts[:, hidden_units:]
    sig = jax.nn.sigmoid(gate)
    swish = gate * sig
    hidden = (swish * upper).astype(jnp.bfloat16)
    y_buf = lax.dot_general(
        hidden, w_out[0], (((1,), (1,)), ((), ())), preferred_element_type=jnp.float32
    ).astype(jnp.bfloat16)
    back = lax.all_to_all(
        y_buf.reshape(n_experts, capacity, width), "expert", split_axis=0, concat_axis=0, tiled=True
    ).reshape(-1, width)
    y_rows = lax.dot_general(
        placing, back, (((0,), (0,)), ((), ())), preferred_element_type=jnp.float32
    )
    output = jnp.sum(
        (gate_flat[:, None] * y_rows).reshape(tok_count, top_count, width), axis=1
    ).astype(jnp.bfloat16)
    got_dy = lax.all_to_all(send_dy, "expert", split_axis=0, concat_axis=0, tiled=True)
    dy_buf = got_dy.reshape(-1, width)
    d_hidden = jnp.dot(dy_buf, w_out[0], preferred_element_type=jnp.float32)
    d_gate = d_hidden * upper * sig * (1.0 + gate * (1.0 - sig))
    d_upper = d_hidden * swish
    d_acts = jnp.concatenate([d_gate, d_upper], axis=1).astype(jnp.bfloat16)
    share = width // n_replicas
    columns = x_buf
    grad_in = lax.psum_scatter(
        lax.dot_general(
            columns, d_acts, (((0,), (0,)), ((), ())), preferred_element_type=jnp.float32
        ).astype(jnp.bfloat16),
        "dp",
        scatter_dimension=0,
        tiled=True,
    ).astype(jnp.float32)
    columns = dy_buf
    grad_out = lax.psum_scatter(
        lax.dot_general(
            columns, hidden, (((0,), (0,)), ((), ())), preferred_element_type=jnp.float32
        ).astype(jnp.bfloat16),
        "dp",
        scatter_dimension=0,
        tiled=True,
    ).astype(jnp.float32)
    return (
        output,
        grad_in.reshape(1, share, 2 * hidden_units),
        grad_out.reshape(1, share, hidden_units),
    )


def solution(mesh):
    in_specs = (
        P(("dp", "expert"), None),
        P(("dp", "expert"), None),
        P(("dp", "expert"), None),
        P(("dp", "expert"), None),
        P("expert", None, None),
        P("expert", None, None),
    )
    out_specs = (P(("dp", "expert"), None), P("expert", "dp", None), P("expert", "dp", None))
    return jax.shard_map(
        on_device, mesh=mesh, in_specs=in_specs, out_specs=out_specs, check_vma=False
    )
```
